128 devices in a mesh: strip: 4 (over y), depth: 32 (over x, z, core).
Axes of the slice: x: 4, y: 4, z: 4, core: 2. Of those that a mesh axis runs over, the one named last changes fastest.
Arguments:
- volume: bfloat16 [256, 128, 2048], P('depth', 'strip'), may hold values from -6 to 6
- occupancy: int32 [32, 4, 16], P('depth', 'strip'), may hold values from 0 to 1
- slab_order: int32 [32], replicated, may hold values from 0 to 31, as said below
- w_in: bfloat16 [4, 64], replicated, may hold values from -3 to 3
- b_in: float32 [64], replicated, may hold values from -3 to 3
- w_out: bfloat16 [64, 4], replicated, may hold values from -1.5 to 1.5
- b_out: float32 [4], replicated, may hold values from -3 to 3
- conv_weight: float32 [3, 3, 3, 3], replicated, may hold values from -1.25 to 1.25
- conv_bias: float32 [3], replicated, may hold values from -3 to 3
Outputs:
- denoised: float32 [3, 4, 1, 32, 2048], P(None, 'strip', None, 'depth')
The draws below stay inside these ranges and needn't reach their ends.
Inputs may be any that keep to these rules, and one draw needn't show every extreme that they name: slab_order is a permutation; for every bit b, bit b of slab_order[d] is bit b of d XOR a value that depends only on d's bits above b (so slabs that agree on their bits above b hold consecutive positions).
All inputs are finite; a program needn't handle non-finite values.
Results may differ from the reference program's by a relative error of at most 0.0003.
Values may be sent and summed in bfloat16 or wider, within the bound.
No kernel may reach another device: no remote copies, remote signals or barrier semaphores. Data moves between devices by JAX's collectives and lax.ppermute only.
A program may use at most 64 MiB of HBM per device.

```python
import jax
import jax.numpy as jnp
from jax import lax

WIDTH = 2048
Z_DEV = 8
CHANNELS = 4
HIDDEN_SIZE = 64
BRICK_ROWS = 32
BRICK_COLS = 128
HEIGHT = 128
DEPTH = 256
ROW_SHARE = 1
N_STRIP = 4
N_DEPTH = 32


def draw_occupancy(key, part):
    level_key = jax.random.fold_in(key, 11)
    value_key = jax.random.fold_in(key, 12)
    levels = jax.random.randint(level_key, (N_DEPTH, 1, 1), 2, 9)
    values = jax.random.randint(value_key, (N_DEPTH, HEIGHT // BRICK_ROWS, WIDTH // BRICK_COLS), 0, 8)
    return (values < levels).astype(jnp.int32)


def draw_slab_order(key, part):
    indices = jnp.arange(N_DEPTH, dtype=jnp.int32)
    order_now = indices
    bit_total = N_DEPTH.bit_length() - 1
    for bit_index in range(bit_total):
        flips = jax.random.randint(jax.random.fold_in(key, 30 + bit_index), (N_DEPTH,), 0, 2).astype(jnp.int32)
        chosen = jnp.take(flips, jnp.right_shift(indices, bit_index + 1))
        order_now = jnp.bitwise_xor(order_now, jnp.left_shift(chosen, bit_index)).astype(jnp.int32)
    return order_now.astype(jnp.int32)


def steps_of(rng, dims, shards, low, high):
    gain = 1.0
    for dim, shards_of in shards:
        draws = jax.random.uniform(jax.random.fold_in(jax.random.fold_in(rng, 6), dim), (shards_of,), jnp.float32, low / len(shards), high / len(shards))
        gain = gain * jnp.repeat(jnp.exp(draws), dims[dim] // shards_of).reshape((-1,) + (1,) * (len(dims) - 1 - dim))
    return gain


def bell_draw(rng, dims, scale, bound, pieces=(), kind=jnp.bfloat16):
    entries = scale * jax.random.normal(rng, dims, jnp.float32)
    if pieces:
        entries = entries * steps_of(rng, dims, pieces, -0.22, 0.18)
    return jnp.clip(entries, -bound, bound).astype(kind)


def setup_inputs(seed: int = 0) -> dict:
    seeds = jax.random.split(jax.random.key(seed), 10)
    volume = bell_draw(seeds[0], (DEPTH, HEIGHT, WIDTH), 1.0, 6.0, ((0, 32), (1, 4)))
    occupancy = draw_occupancy(jax.random.fold_in(seeds[9], 71), 0)
    slab_order = draw_slab_order(jax.random.fold_in(seeds[9], 71), 0)
    w_in = bell_draw(seeds[3], (CHANNELS, HIDDEN_SIZE), CHANNELS ** -0.5, 3.0)
    b_in = bell_draw(seeds[4], (HIDDEN_SIZE,), 0.5, 3.0, (), jnp.float32)
    w_out = bell_draw(seeds[5], (HIDDEN_SIZE, CHANNELS), 0.25, 1.5)
    b_out = bell_draw(seeds[6], (CHANNELS,), 1.0, 3.0, (), jnp.float32)
    conv_weight = bell_draw(seeds[7], (3, 3, 3, 3), 27 ** -0.5, 1.25, (), jnp.float32)
    conv_bias = bell_draw(seeds[8], (3,), 0.5, 3.0, (), jnp.float32)
    return dict(volume=volume, occupancy=occupancy, slab_order=slab_order, w_in=w_in, b_in=b_in, w_out=w_out, b_out=b_out, conv_weight=conv_weight, conv_bias=conv_bias)


def expand_bricks(bricks):
    brick_rows_n, brick_cols_n = bricks.shape
    spread = jnp.broadcast_to(bricks.astype(jnp.float32)[:, None, :, None], (brick_rows_n, BRICK_ROWS, brick_cols_n, BRICK_COLS))
    return spread.reshape(brick_rows_n * BRICK_ROWS, brick_cols_n * BRICK_COLS)


def march_slab(features, coverage, w_in, b_in, w_out, b_out, optical):
    rows_all = features.shape[2]
    cols_all = features.shape[3]

    def layer_step(state_pair, layer_feats):
        colour_sum, remaining = state_pair
        flattened = layer_feats.reshape(4, rows_all * cols_all)
        hidden = jax.nn.silu(jnp.dot(w_in.T, flattened, preferred_element_type=jnp.float32) + b_in[:, None]).astype(jnp.bfloat16)
        output = jnp.dot(w_out.T, hidden, preferred_element_type=jnp.float32) + b_out[:, None]
        output = output.reshape(4, rows_all, cols_all)
        colour = jax.nn.sigmoid(output[:3])
        density = jax.nn.softplus(output[3]) * coverage
        alpha_val = 1.0 - jnp.exp(-optical * density)
        colour_sum = colour_sum + (remaining * alpha_val)[None] * colour
        remaining = remaining * (1.0 - alpha_val)
        return (colour_sum, remaining), None

    start = (jnp.zeros((3, rows_all, cols_all), jnp.float32), jnp.ones((rows_all, cols_all), jnp.float32))
    (colour_sum, remaining), unused = lax.scan(layer_step, start, features)
    return colour_sum, remaining


def slab_features(slab_field):
    scalar_field = slab_field.astype(jnp.float32)
    padded_cols = jnp.pad(scalar_field, ((0, 0), (0, 0), (1, 1)))
    grad_cols = 0.5 * (padded_cols[:, :, 2:] - padded_cols[:, :, :-2])
    padded_rows = jnp.pad(scalar_field, ((0, 0), (1, 1), (0, 0)))
    grad_rows = 0.5 * (padded_rows[:, 2:] - padded_rows[:, :-2])
    padded_depth = jnp.concatenate([scalar_field[:1], scalar_field, scalar_field[-1:]], 0)
    grad_depth = 0.5 * (padded_depth[2:] - padded_depth[:-2])
    return jnp.stack([scalar_field, grad_cols, grad_rows, grad_depth], 1).astype(jnp.bfloat16)


def denoise(picture, conv_weight, conv_bias):
    rows_all = picture.shape[1]
    cols_all = picture.shape[2]
    padded = jnp.pad(picture, ((0, 0), (1, 1), (1, 1)))
    filtered = jnp.broadcast_to(conv_bias[:, None, None], (3, rows_all, cols_all))
    for row_off in range(3):
        for col_off in range(3):
            window = padded[:, row_off:row_off + rows_all, col_off:col_off + cols_all]
            filtered = filtered + jnp.sum(conv_weight[:, :, row_off, col_off][:, :, None, None] * window[None], axis=1)
    return filtered


def reference(volume, occupancy, slab_order, w_in, b_in, w_out, b_out, conv_weight, conv_bias):
    optical = 2.0 / DEPTH
    inverse = jnp.argsort(slab_order).astype(jnp.int32)

    def composite(state_pair, position):
        colour_acc, remaining_acc = state_pair
        slab_index = inverse[position].astype(jnp.int32)
        slab_field = lax.dynamic_slice_in_dim(volume, (slab_index * Z_DEV).astype(jnp.int32), Z_DEV, 0)
        coverage = expand_bricks(lax.dynamic_index_in_dim(occupancy, slab_index, 0, keepdims=False))
        colour_slab, remaining_slab = march_slab(slab_features(slab_field), coverage, w_in, b_in, w_out, b_out, optical)
        return (colour_acc + remaining_acc[None] * colour_slab, remaining_acc * remaining_slab), None

    start = (jnp.zeros((3, HEIGHT, WIDTH), jnp.float32), jnp.ones((HEIGHT, WIDTH), jnp.float32))
    (picture, remaining_end), unused = lax.scan(composite, start, jnp.arange(N_DEPTH, dtype=jnp.int32))
    filtered = denoise(picture, conv_weight, conv_bias)
    return filtered.reshape(3, N_STRIP, ROW_SHARE, N_DEPTH, WIDTH)
```

```python
import functools

import jax
import jax.numpy as jnp
from jax import lax
from jax.experimental import pallas as pl
from jax.experimental.pallas import tpu as pltpu
from jax.sharding import PartitionSpec as P

HIDDEN = 64
KDIM = 48
F32 = jnp.float32
BF16 = jnp.bfloat16


def iota(shape, dim):
    return lax.broadcasted_iota(jnp.int32, shape, dim)


def prepare_weights(w_in, b_in, w_out, w1, w2):
    bias = 0.5 * b_in[...]
    hi = bias.astype(BF16).astype(F32)
    mid = (bias - hi).astype(BF16).astype(F32)
    low = bias - hi - mid
    table = jnp.concatenate(
        [0.5 * w_in[...].astype(F32), hi, mid, low, jnp.zeros((1, HIDDEN), F32)], 0
    ).astype(BF16)
    spread = (iota((HIDDEN * 8, HIDDEN), 0) // 8 == iota((HIDDEN * 8, HIDDEN), 1)).astype(BF16)
    nt = (((1,), (1,)), ((), ()))
    by_row = lax.dot_general(spread, table, nt, preferred_element_type=F32).astype(BF16)
    slot = iota((8, KDIM), 0)
    col = iota((8, KDIM), 1)
    place = jnp.where(col < 32, col // 8, col - 28) == slot
    wide = jnp.dot(by_row, place.astype(BF16), preferred_element_type=F32)
    r = iota((HIDDEN * 8, KDIM), 0)
    k = iota((HIDDEN * 8, KDIM), 1)
    w1[...] = jnp.where((k >= 32) | (r % 8 == k % 8), wide, 0.0).astype(BF16)
    pick = (iota((32, 4), 0) // 8 == iota((32, 4), 1)).astype(BF16)
    out_rows = lax.dot_general(
        pick, w_out[...], (((1,), (1,)), ((), ())), preferred_element_type=F32
    ).astype(BF16)
    full = lax.dot_general(out_rows, spread, nt, preferred_element_type=F32)
    o = iota((32, HIDDEN * 8), 0)
    q = iota((32, HIDDEN * 8), 1)
    scale = jnp.where(o < 24, 0.5, 1.0)
    w2[...] = jnp.where(o % 8 == q % 8, full * scale, 0.0).astype(BF16)


def feature_kernel(vol, top, bot, w_in, b_in, w_out, feats, w1, w2, lines, planes):
    layers, rows, columns = vol.shape
    half = columns // 2
    prepare_weights(w_in, b_in, w_out, w1, w2)

    blocks = half // 128

    def permute(z, carry):
        field = vol[z].astype(F32)
        for k in range(2 * blocks):
            lines[k * rows : (k + 1) * rows] = field[:, k * 128 : (k + 1) * 128]
        for j in range(8):
            for k in range(blocks):
                left = lines[pl.ds(k * rows + j, 4, stride=8)]
                right = lines[pl.ds((k + blocks) * rows + j, 4, stride=8)]
                planes[z, j, :, k * 128 : (k + 1) * 128] = jnp.concatenate([left, right], 0)
        return carry

    lax.fori_loop(0, layers, permute, 0)
    lane = iota((8, half), 1)
    sub = iota((8, half), 0)
    ones = jnp.ones((KDIM - 32, half), BF16)

    def gradients(z, carry):
        before = jnp.maximum(z - 1, 0)
        after = jnp.minimum(z + 1, layers - 1)
        first = jnp.broadcast_to(top[z].astype(F32), (8, columns))
        last = jnp.broadcast_to(bot[z].astype(F32), (8, columns))
        for j in range(8):
            s = planes[z, j]
            ahead = pltpu.roll(s, half - 1, 1)
            behind = pltpu.roll(s, 1, 1)
            ahead = jnp.where(
                lane == half - 1, jnp.where(sub < 4, pltpu.roll(ahead, 4, 0), 0.0), ahead
            )
            behind = jnp.where(lane == 0, jnp.where(sub >= 4, pltpu.roll(behind, 4, 0), 0.0), behind)
            if j > 0:
                above = planes[z, j - 1]
            else:
                above = pltpu.roll(planes[z, 7], 1, 0)
                above = jnp.where(sub == 0, first[:, :half], above)
                above = jnp.where(sub == 4, first[:, half:], above)
            if j < 7:
                below = planes[z, j + 1]
            else:
                below = pltpu.roll(planes[z, 0], 7, 0)
                below = jnp.where(sub == 3, last[:, :half], below)
                below = jnp.where(sub == 7, last[:, half:], below)
            deep = planes[after, j] - planes[before, j]
            block = jnp.concatenate(
                [s, 0.5 * (ahead - behind), 0.5 * (below - above), 0.5 * deep], 0
            )
            feats[j % 2, j // 2, z, 0:32] = block.astype(BF16)
            feats[j % 2, j // 2, z, 32:KDIM] = ones
        return carry

    lax.fori_loop(0, layers, gradients, 0)


def march(feats, w1, w2, b_out, coverage, parity, zpos):
    layers = feats.shape[2]
    half = feats.shape[4]

    def layer(z, state):
        x = feats[parity, zpos, z]
        u = jnp.dot(w1[...], x, preferred_element_type=F32)
        hidden = (u * jnp.tanh(u) + u).astype(BF16)
        e = jnp.dot(w2[...], hidden, preferred_element_type=F32)
        raw = e[24:32] + b_out[3]
        density = jnp.maximum(raw, 0.0) + jnp.log1p(jnp.exp(-jnp.abs(raw)))
        alpha = 1.0 - jnp.exp(coverage * density)
        remaining = state[3]
        share = remaining * alpha
        colours = [
            state[o] + share * (0.5 * jnp.tanh(e[8 * o : 8 * o + 8] + 0.5 * b_out[o]) + 0.5)
            for o in range(3)
        ]
        return (*colours, remaining * (1.0 - alpha))

    zero = jnp.zeros((8, half), F32)
    return lax.fori_loop(0, layers, layer, (zero, zero, zero, zero + 1.0), unroll=2)


def coverage_of(occ, optical, half):
    blocks = half // 128
    sub = iota((8, 128), 0)
    cols = []
    for k in range(blocks):
        left = -optical * occ[k].astype(F32)
        right = -optical * occ[k + blocks].astype(F32)
        cols.append(jnp.where(sub < 4, left, right))
    return jnp.concatenate(cols, 1)


def send_kernel(where, feats, w1, w2, b_out, occ, out, *, optical):
    half = feats.shape[4]
    coverage = coverage_of(occ, optical, half)
    parity = 1 - (where[0] & 1)

    def piece(zpos, carry):
        state = march(feats, w1, w2, b_out, coverage, parity, zpos)
        for o in range(4):
            out[zpos, o] = state[o]
        return carry

    lax.fori_loop(0, 4, piece, 0)


def over(parts, places):
    colours = [None] * 3
    total = None
    for i, part in enumerate(parts):
        light = None
        for j, other in enumerate(parts):
            if j != i:
                factor = jnp.where(places[j] < places[i], other[3], 1.0)
                light = factor if light is None else light * factor
        for o in range(3):
            term = light * part[o]
            colours[o] = term if colours[o] is None else colours[o] + term
        total = part[3] if total is None else total * part[3]
    return (*colours, total)


def keep_kernel(where, order, feats, w1, w2, b_out, occ, received, out, *, optical, step):
    half = feats.shape[4]
    coverage = coverage_of(occ, optical, half)
    d = where[0]
    zpos = ((d >> 1) & 3) ^ step
    state = march(feats, w1, w2, b_out, coverage, d & 1, zpos)
    other = tuple(received[zpos, o] for o in range(4))
    merged = over((state, other), (order[d] & 1, order[d ^ 1] & 1))
    for o in range(4):
        out[o] = merged[o]


def merge_z_kernel(where, order, part0, part1, part2, part3, out0, out1, out2, out3):
    d = where[0]
    parts = [tuple(p[o] for o in range(4)) for p in (part0, part1, part2, part3)]
    places = [(order[d ^ (k << 1)] >> 1) & 3 for k in range(4)]
    merged = over(parts, places)
    xpos = d >> 3
    for k, out in enumerate((out0, out1, out2, out3)):
        shift = (8 - (xpos ^ k)) % 8
        for o in range(4):
            turned = pltpu.roll(merged[o], shift, 0)
            out[o] = jnp.concatenate([turned[0:1], turned[4:5]], 0)


def merge_x_kernel(where, order, part0, part1, part2, part3, out):
    d = where[0]
    parts = [tuple(p[o] for o in range(4)) for p in (part0, part1, part2, part3)]
    places = [order[d ^ (k << 3)] >> 3 for k in range(4)]
    merged = over(parts, places)
    for o in range(3):
        out[o] = merged[o]


def filter_kernel(weight, bias, above, centre, below, out):
    half = centre.shape[2]
    lane = iota((2, half), 1)
    sub = iota((2, half), 0)
    sums = [jnp.full((2, half), bias[o], F32) for o in range(3)]
    for i in range(3):
        for a, rows in enumerate((above, centre, below)):
            row = rows[i]
            flipped = jnp.concatenate([row[1:2], row[0:1]], 0)
            left = jnp.where(
                lane == 0, jnp.where(sub == 1, pltpu.roll(flipped, 1, 1), 0.0), pltpu.roll(row, 1, 1)
            )
            right = jnp.where(
                lane == half - 1,
                jnp.where(sub == 0, pltpu.roll(flipped, half - 1, 1), 0.0),
                pltpu.roll(row, half - 1, 1),
            )
            for b, window in enumerate((left, row, right)):
                for o in range(3):
                    sums[o] = sums[o] + weight[((o * 3 + i) * 3 + a) * 3 + b] * window
    for o in range(3):
        out[o, :, :half] = sums[o][0:1]
        out[o, :, half:] = sums[o][1:2]


VMEM = pl.BlockSpec(memory_space=pltpu.VMEM)
SMEM = pl.BlockSpec(memory_space=pltpu.SMEM)


def call(kernel, name, outs, specs, *args, scratch=()):
    return pl.pallas_call(
        kernel,
        out_shape=outs,
        in_specs=specs,
        out_specs=jax.tree.map(lambda _: VMEM, outs),
        scratch_shapes=scratch,
        compiler_params=pltpu.CompilerParams(vmem_limit_bytes=40 * 2**20),
        name=name,
    )(*args)


def shape(dims, dtype=F32):
    return jax.ShapeDtypeStruct(dims, dtype)


def shards(volume, occupancy, slab_order, w_in, b_in, w_out, b_out, conv_weight, conv_bias):
    strips = lax.axis_size("strip")
    depths = lax.axis_size("depth")
    layers, rows, columns = volume.shape
    half = columns // 2
    optical = 2.0 / (layers * depths)
    d = lax.axis_index("depth")
    where = d.astype(jnp.int32).reshape(1)
    down = [(i, i + 1) for i in range(strips - 1)]
    up = [(i + 1, i) for i in range(strips - 1)]
    top = lax.ppermute(volume[:, rows - 1 :], "strip", down)
    bot = lax.ppermute(volume[:, :1], "strip", up)
    feats, w1, w2 = call(
        feature_kernel,
        "features",
        (
            shape((2, 4, layers, KDIM, half), BF16),
            shape((HIDDEN * 8, KDIM), BF16),
            shape((32, HIDDEN * 8), BF16),
        ),
        [VMEM] * 6,
        volume,
        top,
        bot,
        w_in,
        b_in.reshape(1, HIDDEN),
        w_out,
        scratch=[pltpu.VMEM((rows * columns // 128, 128), F32), pltpu.VMEM((layers, 8, 8, half), F32)],
    )
    occ = occupancy.reshape(-1)
    net = (feats, w1, w2, b_out, occ)
    net_specs = [VMEM, VMEM, VMEM, SMEM, SMEM]
    sent = call(
        functools.partial(send_kernel, optical=optical),
        "march_send",
        shape((4, 4, 8, half)),
        [SMEM] + net_specs,
        where,
        *net,
    )
    received = lax.ppermute(sent, "depth", [(i, i ^ 1) for i in range(depths)])
    parts = [None] * 4
    for step in (1, 2, 3, 0):
        piece = call(
            functools.partial(keep_kernel, optical=optical, step=step),
            f"march_keep{step}",
            shape((4, 8, half)),
            [SMEM, SMEM] + net_specs + [VMEM],
            where,
            slab_order,
            *net,
            received,
        )
        if step:
            piece = lax.ppermute(piece, "depth", [(i, i ^ (step << 1)) for i in range(depths)])
        parts[step] = piece
    quads = call(
        merge_z_kernel,
        "merge_z",
        tuple(shape((4, 2, half)) for _ in range(4)),
        [SMEM, SMEM] + [VMEM] * 4,
        where,
        slab_order,
        *parts,
    )
    quads = [
        lax.ppermute(quads[k], "depth", [(i, i ^ (k << 3)) for i in range(depths)]) if k else quads[0]
        for k in range(4)
    ]
    picture = call(
        merge_x_kernel,
        "merge_x",
        shape((3, 2, half)),
        [SMEM, SMEM] + [VMEM] * 4,
        where,
        slab_order,
        *quads,
    )
    count = strips * depths
    above = lax.ppermute(picture, ("strip", "depth"), [(i, i + 1) for i in range(count - 1)])
    below = lax.ppermute(picture, ("strip", "depth"), [(i + 1, i) for i in range(count - 1)])
    filtered = call(
        filter_kernel,
        "filter",
        shape((3, 1, columns)),
        [SMEM, SMEM] + [VMEM] * 3,
        conv_weight.reshape(-1),
        conv_bias,
        above,
        picture,
        below,
    )
    return filtered.reshape(3, 1, 1, 1, columns)


def solution(mesh):
    placed = (
        P("depth", "strip", None),
        P("depth", "strip", None),
        P(),
        P(),
        P(),
        P(),
        P(),
        P(),
        P(),
    )
    return jax.shard_map(
        shards,
        mesh=mesh,
        in_specs=placed,
        out_specs=P(None, "strip", None, "depth", None),
        check_vma=False,
    )
```

```python
import functools

import jax
import jax.numpy as jnp
from jax import lax
from jax.experimental import pallas as pl
from jax.experimental.pallas import tpu as pltpu
from jax.sharding import PartitionSpec as P

HIDDEN = 64
KDIM = 48
F32 = jnp.float32
BF16 = jnp.bfloat16


def iota(shape, dim):
    return lax.broadcasted_iota(jnp.int32, shape, dim)


def prepare_weights(facts, w1, w2):
    bias = 0.5 * facts[4:5]
    hi = bias.astype(BF16).astype(F32)
    mid = (bias - hi).astype(BF16).astype(F32)
    low = bias - hi - mid
    table = jnp.concatenate(
        [0.5 * facts[0:4], hi, mid, low, jnp.zeros((1, HIDDEN), F32)], 0
    ).astype(BF16)
    spread = (iota((HIDDEN * 8, HIDDEN), 0) // 8 == iota((HIDDEN * 8, HIDDEN), 1)).astype(BF16)
    nt = (((1,), (1,)), ((), ()))
    by_row = lax.dot_general(spread, table, nt, preferred_element_type=F32).astype(BF16)
    slot = iota((8, KDIM), 0)
    col = iota((8, KDIM), 1)
    place = jnp.where(col < 32, col // 8, col - 28) == slot
    wide = jnp.dot(by_row, place.astype(BF16), preferred_element_type=F32)
    r = iota((HIDDEN * 8, KDIM), 0)
    k = iota((HIDDEN * 8, KDIM), 1)
    w1[...] = jnp.where((k >= 32) | (r % 8 == k % 8), wide, 0.0).astype(BF16)
    pick = (iota((32, 4), 0) // 8 == iota((32, 4), 1)).astype(BF16)
    out_rows = lax.dot_general(
        pick, facts[5:9].astype(BF16), (((1,), (0,)), ((), ())), preferred_element_type=F32
    ).astype(BF16)
    full = lax.dot_general(out_rows, spread, nt, preferred_element_type=F32)
    o = iota((32, HIDDEN * 8), 0)
    q = iota((32, HIDDEN * 8), 1)
    scale = jnp.where(o < 24, 0.5, 1.0)
    w2[...] = jnp.where(o % 8 == q % 8, full * scale, 0.0).astype(BF16)


def feature_kernel(
    vol, facts, feats, w1, w2, coverage, shift, lines, planes, *, optical
):
    layers, rows, columns = vol.shape
    half = columns // 2
    prepare_weights(facts, w1, w2)
    coverage[...] = coverage_of(facts[10:11], optical, half)
    for o in range(4):
        scale = 0.5 if o < 3 else 1.0
        shift[8 * o : 8 * o + 8] = jnp.broadcast_to(scale * facts[9:10, o : o + 1], (8, 128))
    blocks = half // 128

    def permute(z, carry):
        field = vol[z].astype(F32)
        for k in range(2 * blocks):
            lines[k * rows : (k + 1) * rows] = field[:, k * 128 : (k + 1) * 128]
        for j in range(8):
            for k in range(blocks):
                left = lines[pl.ds(k * rows + j, 4, stride=8)]
                right = lines[pl.ds((k + blocks) * rows + j, 4, stride=8)]
                planes[z, j, :, k * 128 : (k + 1) * 128] = jnp.concatenate([left, right], 0)
        return carry

    lax.fori_loop(0, layers, permute, 0)
    lane = iota((8, half), 1)
    sub = iota((8, half), 0)
    ones = jnp.ones((KDIM - 32, half), BF16)

    def gradients(z, carry):
        before = jnp.maximum(z - 1, 0)
        after = jnp.minimum(z + 1, layers - 1)
        for j in range(8):
            s = planes[z, j]
            ahead = pltpu.roll(s, half - 1, 1)
            behind = pltpu.roll(s, 1, 1)
            ahead = jnp.where(
                lane == half - 1, jnp.where(sub < 4, pltpu.roll(ahead, 4, 0), 0.0), ahead
            )
            behind = jnp.where(lane == 0, jnp.where(sub >= 4, pltpu.roll(behind, 4, 0), 0.0), behind)
            if j > 0:
                above = planes[z, j - 1]
            else:
                above = pltpu.roll(planes[z, 7], 1, 0)
            if j < 7:
                below = planes[z, j + 1]
            else:
                below = pltpu.roll(planes[z, 0], 7, 0)
            deep = planes[after, j] - planes[before, j]
            block = jnp.concatenate(
                [s, 0.5 * (ahead - behind), 0.5 * (below - above), 0.5 * deep], 0
            )
            feats[j % 2, j // 2, z, 0:32] = block.astype(BF16)
            feats[j % 2, j // 2, z, 32:KDIM] = ones
        return carry

    lax.fori_loop(0, layers, gradients, 0)


def edge_kernel(feats, top, bot, after, edges):
    layers = feats.shape[2]
    half = feats.shape[4]
    sub = iota((8, half), 0)

    def fix(z, carry):
        for parity, zpos, rim, low in ((0, 0, top, 0), (1, 3, bot, 3)):
            inner = feats[1 - parity, zpos, z, 0:16].astype(F32)[0:8]
            both = feats[parity, zpos, z, 16:32].astype(F32)
            line = rim[z].astype(F32)
            outer = jnp.where(sub < 4, line[:, :half], line[:, half:])
            slope = 0.5 * (inner - outer) if parity == 0 else 0.5 * (outer - inner)
            fixed = jnp.where(sub % 4 == low, slope, both[0:8])
            edges[parity, z, 0:16] = feats[parity, zpos, z, 0:16]
            edges[parity, z, 16:32] = jnp.concatenate([fixed, both[8:16]], 0).astype(BF16)
            edges[parity, z, 32:KDIM] = feats[parity, zpos, z, 32:KDIM]
        return carry

    lax.fori_loop(0, layers, fix, 0)


def load_plane(feats, edges, parity, zpos, x):
    at_edge = zpos == 3 * parity

    @pl.when(at_edge)
    def _():
        x[...] = edges[parity]

    @pl.when(jnp.logical_not(at_edge))
    def _():
        x[...] = feats[parity, zpos]


def march(plane, w1, w2, coverage, shift):
    layers, _, half = plane.shape
    cover = coverage[...]
    lift = jnp.concatenate([shift[...]] * (half // 128), 1)

    def layer(z, state):
        x = plane[z]
        u = jnp.dot(w1[...], x, preferred_element_type=F32)
        hidden = (u * jnp.tanh(u) + u).astype(BF16)
        e = jnp.dot(w2[...], hidden, preferred_element_type=F32) + lift
        raw = e[24:32]
        density = jnp.maximum(raw, 0.0) + jnp.log1p(jnp.exp(-jnp.abs(raw)))
        alpha = 1.0 - jnp.exp(cover * density)
        remaining = state[3]
        share = remaining * alpha
        colours = [
            state[o] + share * (0.5 * jnp.tanh(e[8 * o : 8 * o + 8]) + 0.5) for o in range(3)
        ]
        return (*colours, remaining * (1.0 - alpha))

    zero = jnp.zeros((8, half), F32)
    return lax.fori_loop(0, layers, layer, (zero, zero, zero, zero + 1.0), unroll=2)


def coverage_of(occ, optical, half):
    blocks = half // 128
    sub = iota((8, 128), 0)
    scaled = -optical * occ
    cols = []
    for k in range(blocks):
        left = jnp.broadcast_to(scaled[:, k : k + 1], (8, 128))
        right = jnp.broadcast_to(scaled[:, k + blocks : k + blocks + 1], (8, 128))
        cols.append(jnp.where(sub < 4, left, right))
    return jnp.concatenate(cols, 1)


def send_inner_kernel(where, feats, w1, w2, coverage, shift, out):
    parity = 1 - (where[0] & 1)

    def piece(i, carry):
        state = march(feats.at[parity, 1 + i], w1, w2, coverage, shift)
        for o in range(4):
            out[i, o] = state[o]
        return carry

    lax.fori_loop(0, 2, piece, 0)


def send_outer_kernel(where, feats, edges, w1, w2, coverage, shift, out, x):
    parity = 1 - (where[0] & 1)

    def piece(i, carry):
        load_plane(feats, edges, parity, 3 * i, x)
        state = march(x, w1, w2, coverage, shift)
        for o in range(4):
            out[i, o] = state[o]
        return carry

    lax.fori_loop(0, 2, piece, 0)


def over(parts, places):
    colours = [None] * 3
    total = None
    for i, part in enumerate(parts):
        light = None
        for j, other in enumerate(parts):
            if j != i:
                factor = jnp.where(places[j] < places[i], other[3], 1.0)
                light = factor if light is None else light * factor
        for o in range(3):
            term = light * part[o]
            colours[o] = term if colours[o] is None else colours[o] + term
        total = part[3] if total is None else total * part[3]
    return (*colours, total)


def keep_kernel(
    where, order, feats, edges, w1, w2, coverage, shift, inner, outer, out, x, *, step
):
    d = where[0]
    zpos = ((d >> 1) & 3) ^ step
    load_plane(feats, edges, d & 1, zpos, x)
    state = march(x, w1, w2, coverage, shift)
    slot = zpos >> 1
    middle = (zpos == 1) | (zpos == 2)
    other = tuple(jnp.where(middle, inner[slot, o], outer[slot, o]) for o in range(4))
    merged = over((state, other), (order[d] & 1, order[d ^ 1] & 1))
    for o in range(4):
        out[o] = merged[o]


def merge_z_kernel(where, order, part0, part1, part2, part3, out0, out1, out2, out3):
    d = where[0]
    parts = [tuple(p[o] for o in range(4)) for p in (part0, part1, part2, part3)]
    places = [(order[d ^ (k << 1)] >> 1) & 3 for k in range(4)]
    merged = over(parts, places)
    xpos = d >> 3
    for k, out in enumerate((out0, out1, out2, out3)):
        shift = (8 - (xpos ^ k)) % 8
        for o in range(4):
            turned = pltpu.roll(merged[o], shift, 0)
            out[o] = jnp.concatenate([turned[0:1], turned[4:5]], 0)


def merge_x_kernel(where, order, part0, part1, part2, part3, out):
    d = where[0]
    parts = [tuple(p[o] for o in range(4)) for p in (part0, part1, part2, part3)]
    places = [order[d ^ (k << 3)] >> 3 for k in range(4)]
    merged = over(parts, places)
    for o in range(3):
        out[o] = merged[o]


def filter_kernel(where, weight, bias, beside, centre, apart, out):
    half = centre.shape[2]
    even = (where[0] & 1) == 0
    lane = iota((2, half), 1)
    sub = iota((2, half), 0)
    sums = [jnp.full((2, half), bias[o], F32) for o in range(3)]
    for i in range(3):
        above = jnp.where(even, apart[i], beside[i])
        below = jnp.where(even, beside[i], apart[i])
        for a, row in enumerate((above, centre[i], below)):
            flipped = jnp.concatenate([row[1:2], row[0:1]], 0)
            left = jnp.where(
                lane == 0, jnp.where(sub == 1, pltpu.roll(flipped, 1, 1), 0.0), pltpu.roll(row, 1, 1)
            )
            right = jnp.where(
                lane == half - 1,
                jnp.where(sub == 0, pltpu.roll(flipped, half - 1, 1), 0.0),
                pltpu.roll(row, half - 1, 1),
            )
            for b, window in enumerate((left, row, right)):
                for o in range(3):
                    sums[o] = sums[o] + weight[((o * 3 + i) * 3 + a) * 3 + b] * window
    for o in range(3):
        out[o, :, :half] = sums[o][0:1]
        out[o, :, half:] = sums[o][1:2]


VMEM = pl.BlockSpec(memory_space=pltpu.VMEM)
SMEM = pl.BlockSpec(memory_space=pltpu.SMEM)


def call(kernel, name, outs, specs, *args, scratch=()):
    return pl.pallas_call(
        kernel,
        out_shape=outs,
        in_specs=specs,
        out_specs=jax.tree.map(lambda _: VMEM, outs),
        scratch_shapes=scratch,
        compiler_params=pltpu.CompilerParams(vmem_limit_bytes=24 * 2**20),
        name=name,
    )(*args)


def shape(dims, dtype=F32):
    return jax.ShapeDtypeStruct(dims, dtype)


def shards(volume, occupancy, slab_order, w_in, b_in, w_out, b_out, conv_weight, conv_bias):
    strips = lax.axis_size("strip")
    depths = lax.axis_size("depth")
    layers, rows, columns = volume.shape
    half = columns // 2
    optical = 2.0 / (layers * depths)
    d = lax.axis_index("depth")
    where = d.astype(jnp.int32).reshape(1)
    wide = lambda v: jnp.pad(v.astype(F32).reshape(1, -1), ((0, 0), (0, HIDDEN - v.size)))
    facts = jnp.concatenate(
        [w_in.astype(F32), wide(b_in), w_out.T.astype(F32), wide(b_out), wide(occupancy)], 0
    )
    feats, w1, w2, coverage, shift = call(
        functools.partial(feature_kernel, optical=optical),
        "features",
        (
            shape((2, 4, layers, KDIM, half), BF16),
            shape((HIDDEN * 8, KDIM), BF16),
            shape((32, HIDDEN * 8), BF16),
            shape((8, half)),
            shape((32, 128)),
        ),
        [VMEM] * 2,
        volume,
        facts,
        scratch=[
            pltpu.VMEM((rows * columns // 128, 128), F32),
            pltpu.VMEM((layers, 8, 8, half), F32),
        ],
    )
    top = lax.ppermute(volume[:, rows - 1 :], "strip", [(i, i + 1) for i in range(strips - 1)])
    bot = lax.ppermute(volume[:, :1], "strip", [(i + 1, i) for i in range(strips - 1)])
    net = (w1, w2, coverage, shift)
    cores = [(i, i ^ 1) for i in range(depths)]
    sent = call(
        send_inner_kernel,
        "march_send_inner",
        shape((2, 4, 8, half)),
        [SMEM] + [VMEM] * 5,
        where,
        feats,
        *net,
    )
    inner = lax.ppermute(sent, "depth", cores)
    edges = call(
        edge_kernel,
        "edges",
        shape((2, layers, KDIM, half), BF16),
        [VMEM] * 3 + [pl.BlockSpec(memory_space=pl.ANY)],
        feats,
        top,
        bot,
        sent,
    )
    plane = pltpu.VMEM((layers, KDIM, half), BF16)
    sent = call(
        send_outer_kernel,
        "march_send_outer",
        shape((2, 4, 8, half)),
        [SMEM] + [VMEM] * 6,
        where,
        feats,
        edges,
        *net,
        scratch=[plane],
    )
    outer = lax.ppermute(sent, "depth", cores)
    parts = [None] * 4
    for step in (1, 2, 3, 0):
        piece = call(
            functools.partial(keep_kernel, step=step),
            f"march_keep{step}",
            shape((4, 8, half)),
            [SMEM, SMEM] + [VMEM] * 8,
            where,
            slab_order,
            feats,
            edges,
            *net,
            inner,
            outer,
            scratch=[plane],
        )
        if step:
            piece = lax.ppermute(piece, "depth", [(i, i ^ (step << 1)) for i in range(depths)])
        parts[step] = piece
    quads = call(
        merge_z_kernel,
        "merge_z",
        tuple(shape((4, 2, half)) for _ in range(4)),
        [SMEM, SMEM] + [VMEM] * 4,
        where,
        slab_order,
        *parts,
    )
    quads = [
        lax.ppermute(quads[k], "depth", [(i, i ^ (k << 3)) for i in range(depths)]) if k else quads[0]
        for k in range(4)
    ]
    picture = call(
        merge_x_kernel,
        "merge_x",
        shape((3, 2, half)),
        [SMEM, SMEM] + [VMEM] * 4,
        where,
        slab_order,
        *quads,
    )
    pairs = [(i, i + 1) for i in range(1, strips * depths - 1, 2)]
    apart = lax.ppermute(picture, ("strip", "depth"), pairs + [(j, i) for i, j in pairs])
    beside = lax.ppermute(picture, "depth", cores)
    filtered = call(
        filter_kernel,
        "filter",
        shape((3, 1, columns)),
        [SMEM] * 3 + [VMEM] * 3,
        where,
        conv_weight.reshape(-1),
        conv_bias,
        beside,
        picture,
        apart,
    )
    return filtered.reshape(3, 1, 1, 1, columns)


def solution(mesh):
    placed = (
        P("depth", "strip", None),
        P("depth", "strip", None),
        P(),
        P(),
        P(),
        P(),
        P(),
        P(),
        P(),
    )
    return jax.shard_map(
        shards,
        mesh=mesh,
        in_specs=placed,
        out_specs=P(None, "strip", None, "depth", None),
        check_vma=False,
    )
```

```python
import functools

import jax
import jax.numpy as jnp
from jax import lax
from jax.experimental import pallas as pl
from jax.experimental.pallas import tpu as pltpu
from jax.sharding import PartitionSpec as P

HIDDEN = 64
KDIM = 48
CHUNK = 256
LAG = 2
F32 = jnp.float32
BF16 = jnp.bfloat16


def iota(shape, dim):
    return lax.broadcasted_iota(jnp.int32, shape, dim)


def prepare_weights(facts, w1, w2):
    bias = 0.5 * facts[4:5]
    hi = bias.astype(BF16).astype(F32)
    mid = (bias - hi).astype(BF16).astype(F32)
    low = bias - hi - mid
    table = jnp.concatenate(
        [0.5 * facts[0:4], hi, mid, low, jnp.zeros((1, HIDDEN), F32)], 0
    ).astype(BF16)
    spread = (iota((HIDDEN * 8, HIDDEN), 0) // 8 == iota((HIDDEN * 8, HIDDEN), 1)).astype(BF16)
    nt = (((1,), (1,)), ((), ()))
    by_row = lax.dot_general(spread, table, nt, preferred_element_type=F32).astype(BF16)
    slot = iota((8, KDIM), 0)
    col = iota((8, KDIM), 1)
    place = jnp.where(col < 32, col // 8, col - 28) == slot
    wide = jnp.dot(by_row, place.astype(BF16), preferred_element_type=F32)
    r = iota((HIDDEN * 8, KDIM), 0)
    k = iota((HIDDEN * 8, KDIM), 1)
    w1[...] = jnp.where((k >= 32) | (r % 8 == k % 8), wide, 0.0).astype(BF16)
    pick = (iota((32, 4), 0) // 8 == iota((32, 4), 1)).astype(BF16)
    out_rows = lax.dot_general(
        pick, facts[5:9].astype(BF16), (((1,), (0,)), ((), ())), preferred_element_type=F32
    ).astype(BF16)
    full = lax.dot_general(out_rows, spread, nt, preferred_element_type=F32)
    o = iota((32, HIDDEN * 8), 0)
    q = iota((32, HIDDEN * 8), 1)
    scale = jnp.where(o < 24, 0.5, 1.0)
    w2[...] = jnp.where(o % 8 == q % 8, full * scale, 0.0).astype(BF16)


def feature_kernel(
    vol, facts, feats, w1, w2, coverage, shift, lines, planes, *, optical
):
    layers, rows, columns = vol.shape
    half = columns // 2
    prepare_weights(facts, w1, w2)
    coverage[...] = coverage_of(facts[10:11], optical, half)
    for o in range(4):
        scale = 0.5 if o < 3 else 1.0
        shift[8 * o : 8 * o + 8] = jnp.broadcast_to(scale * facts[9:10, o : o + 1], (8, 128))
    blocks = half // 128

    def permute(z, carry):
        field = vol[z].astype(F32)
        for k in range(2 * blocks):
            lines[k * rows : (k + 1) * rows] = field[:, k * 128 : (k + 1) * 128]
        for j in range(8):
            for k in range(blocks):
                left = lines[pl.ds(k * rows + j, 4, stride=8)]
                right = lines[pl.ds((k + blocks) * rows + j, 4, stride=8)]
                planes[z, j, :, k * 128 : (k + 1) * 128] = jnp.concatenate([left, right], 0)
        return carry

    lax.fori_loop(0, layers, permute, 0)
    lane = iota((8, half), 1)
    sub = iota((8, half), 0)
    ones = jnp.ones((KDIM - 32, half), BF16)

    def gradients(z, carry):
        before = jnp.maximum(z - 1, 0)
        after = jnp.minimum(z + 1, layers - 1)
        for j in range(8):
            s = planes[z, j]
            ahead = pltpu.roll(s, half - 1, 1)
            behind = pltpu.roll(s, 1, 1)
            ahead = jnp.where(
                lane == half - 1, jnp.where(sub < 4, pltpu.roll(ahead, 4, 0), 0.0), ahead
            )
            behind = jnp.where(lane == 0, jnp.where(sub >= 4, pltpu.roll(behind, 4, 0), 0.0), behind)
            if j > 0:
                above = planes[z, j - 1]
            else:
                above = pltpu.roll(planes[z, 7], 1, 0)
            if j < 7:
                below = planes[z, j + 1]
            else:
                below = pltpu.roll(planes[z, 0], 7, 0)
            deep = planes[after, j] - planes[before, j]
            block = jnp.concatenate(
                [s, 0.5 * (ahead - behind), 0.5 * (below - above), 0.5 * deep], 0
            )
            feats[j % 2, j // 2, z, 0:32] = block.astype(BF16)
            feats[j % 2, j // 2, z, 32:KDIM] = ones
        return carry

    lax.fori_loop(0, layers, gradients, 0)


def edge_kernel(feats, top, bot, after, edges):
    layers = feats.shape[2]
    half = feats.shape[4]
    sub = iota((8, half), 0)

    def fix(z, carry):
        for parity, zpos, rim, low in ((0, 0, top, 0), (1, 3, bot, 3)):
            inner = feats[1 - parity, zpos, z, 0:16].astype(F32)[0:8]
            both = feats[parity, zpos, z, 16:32].astype(F32)
            line = rim[z].astype(F32)
            outer = jnp.where(sub < 4, line[:, :half], line[:, half:])
            slope = 0.5 * (inner - outer) if parity == 0 else 0.5 * (outer - inner)
            fixed = jnp.where(sub % 4 == low, slope, both[0:8])
            edges[parity, z, 0:16] = feats[parity, zpos, z, 0:16]
            edges[parity, z, 16:32] = jnp.concatenate([fixed, both[8:16]], 0).astype(BF16)
            edges[parity, z, 32:KDIM] = feats[parity, zpos, z, 32:KDIM]
        return carry

    lax.fori_loop(0, layers, fix, 0)


def load_plane(feats, edges, parity, zpos, x):
    at_edge = zpos == 3 * parity

    @pl.when(at_edge)
    def _():
        x[...] = edges[parity]

    @pl.when(jnp.logical_not(at_edge))
    def _():
        x[...] = feats[parity, zpos]


def march(plane, w1, w2, coverage, shift, out):
    layers, _, half = plane.shape
    lift = jnp.concatenate([shift[...]] * (CHUNK // 128), 1)
    steps = [(c, z) for c in range(0, half, CHUNK) for z in range(layers)]
    waiting = []
    states = {}
    for n in range(len(steps) + LAG):
        if n < len(steps):
            c, z = steps[n]
            u = jnp.dot(w1[...], plane[z, :, c : c + CHUNK], preferred_element_type=F32)
            waiting.append((u * jnp.tanh(u) + u).astype(BF16))
        if n < LAG:
            continue
        c, z = steps[n - LAG]
        e = jnp.dot(w2[...], waiting[n - LAG], preferred_element_type=F32) + lift
        waiting[n - LAG] = None
        raw = e[24:32]
        density = jnp.maximum(raw, 0.0) + jnp.log1p(jnp.exp(-jnp.abs(raw)))
        alpha = 1.0 - jnp.exp(coverage[:, c : c + CHUNK] * density)
        colours = [0.5 * jnp.tanh(e[8 * o : 8 * o + 8]) + 0.5 for o in range(3)]
        if z == 0:
            state = [alpha * colour for colour in colours] + [1.0 - alpha]
        else:
            share = states[c][3] * alpha
            state = [states[c][o] + share * colours[o] for o in range(3)]
            state.append(states[c][3] * (1.0 - alpha))
        states[c] = state
        if z == layers - 1:
            for o in range(4):
                out[o, :, c : c + CHUNK] = states[c][o]


def coverage_of(occ, optical, half):
    blocks = half // 128
    sub = iota((8, 128), 0)
    scaled = -optical * occ
    cols = []
    for k in range(blocks):
        left = jnp.broadcast_to(scaled[:, k : k + 1], (8, 128))
        right = jnp.broadcast_to(scaled[:, k + blocks : k + blocks + 1], (8, 128))
        cols.append(jnp.where(sub < 4, left, right))
    return jnp.concatenate(cols, 1)


def send_inner_kernel(where, feats, w1, w2, coverage, shift, out):
    parity = 1 - (where[0] & 1)

    def piece(i, carry):
        march(feats.at[parity, 1 + i], w1, w2, coverage, shift, out.at[i])
        return carry

    lax.fori_loop(0, 2, piece, 0)


def send_outer_kernel(where, feats, edges, w1, w2, coverage, shift, out, x):
    parity = 1 - (where[0] & 1)

    def piece(i, carry):
        load_plane(feats, edges, parity, 3 * i, x)
        march(x, w1, w2, coverage, shift, out.at[i])
        return carry

    lax.fori_loop(0, 2, piece, 0)


def over(parts, places):
    colours = [None] * 3
    total = None
    for i, part in enumerate(parts):
        light = None
        for j, other in enumerate(parts):
            if j != i:
                factor = jnp.where(places[j] < places[i], other[3], 1.0)
                light = factor if light is None else light * factor
        for o in range(3):
            term = light * part[o]
            colours[o] = term if colours[o] is None else colours[o] + term
        total = part[3] if total is None else total * part[3]
    return (*colours, total)


def keep_kernel(
    where, order, feats, edges, w1, w2, coverage, shift, inner, outer, out, x, *, step
):
    d = where[0]
    zpos = ((d >> 1) & 3) ^ step
    load_plane(feats, edges, d & 1, zpos, x)
    march(x, w1, w2, coverage, shift, out)
    state = tuple(out[o] for o in range(4))
    slot = zpos >> 1
    middle = (zpos == 1) | (zpos == 2)
    other = tuple(jnp.where(middle, inner[slot, o], outer[slot, o]) for o in range(4))
    merged = over((state, other), (order[d] & 1, order[d ^ 1] & 1))
    for o in range(4):
        out[o] = merged[o]


def merge_z_kernel(where, order, part0, part1, part2, part3, out0, out1, out2, out3):
    d = where[0]
    parts = [tuple(p[o] for o in range(4)) for p in (part0, part1, part2, part3)]
    places = [(order[d ^ (k << 1)] >> 1) & 3 for k in range(4)]
    merged = over(parts, places)
    xpos = d >> 3
    for k, out in enumerate((out0, out1, out2, out3)):
        shift = (8 - (xpos ^ k)) % 8
        for o in range(4):
            turned = pltpu.roll(merged[o], shift, 0)
            out[o] = jnp.concatenate([turned[0:1], turned[4:5]], 0)


def merge_x_kernel(where, order, part0, part1, part2, part3, out):
    d = where[0]
    parts = [tuple(p[o] for o in range(4)) for p in (part0, part1, part2, part3)]
    places = [order[d ^ (k << 3)] >> 3 for k in range(4)]
    merged = over(parts, places)
    for o in range(3):
        out[o] = merged[o]


def filter_kernel(where, weight, bias, beside, centre, apart, out):
    half = centre.shape[2]
    even = (where[0] & 1) == 0
    lane = iota((2, half), 1)
    sub = iota((2, half), 0)
    sums = [jnp.full((2, half), bias[o], F32) for o in range(3)]
    for i in range(3):
        above = jnp.where(even, apart[i], beside[i])
        below = jnp.where(even, beside[i], apart[i])
        for a, row in enumerate((above, centre[i], below)):
            flipped = jnp.concatenate([row[1:2], row[0:1]], 0)
            left = jnp.where(
                lane == 0, jnp.where(sub == 1, pltpu.roll(flipped, 1, 1), 0.0), pltpu.roll(row, 1, 1)
            )
            right = jnp.where(
                lane == half - 1,
                jnp.where(sub == 0, pltpu.roll(flipped, half - 1, 1), 0.0),
                pltpu.roll(row, half - 1, 1),
            )
            for b, window in enumerate((left, row, right)):
                for o in range(3):
                    sums[o] = sums[o] + weight[((o * 3 + i) * 3 + a) * 3 + b] * window
    for o in range(3):
        out[o, :, :half] = sums[o][0:1]
        out[o, :, half:] = sums[o][1:2]


VMEM = pl.BlockSpec(memory_space=pltpu.VMEM)
SMEM = pl.BlockSpec(memory_space=pltpu.SMEM)


def call(kernel, name, outs, specs, *args, scratch=()):
    return pl.pallas_call(
        kernel,
        out_shape=outs,
        in_specs=specs,
        out_specs=jax.tree.map(lambda _: VMEM, outs),
        scratch_shapes=scratch,
        compiler_params=pltpu.CompilerParams(vmem_limit_bytes=24 * 2**20),
        name=name,
    )(*args)


def shape(dims, dtype=F32):
    return jax.ShapeDtypeStruct(dims, dtype)


def table_of(*arrays):
    flat = [v.astype(F32).reshape(-1, v.shape[-1]) for v in arrays]
    rows = sum(v.shape[0] for v in flat)
    total, at = 0.0, 0
    for v in flat:
        n, width = v.shape
        total = total + jnp.pad(v, ((at, rows - at - n), (0, HIDDEN - width)))
        at += n
    return total


def shards(volume, occupancy, slab_order, w_in, b_in, w_out, b_out, conv_weight, conv_bias):
    strips = lax.axis_size("strip")
    depths = lax.axis_size("depth")
    layers, rows, columns = volume.shape
    half = columns // 2
    optical = 2.0 / (layers * depths)
    d = lax.axis_index("depth")
    where = d.astype(jnp.int32).reshape(1)
    facts = table_of(w_in, b_in, w_out.T, b_out, occupancy)
    top = lax.ppermute(volume[:, rows - 1 :], "strip", [(i, i + 1) for i in range(strips - 1)])
    bot = lax.ppermute(volume[:, :1], "strip", [(i + 1, i) for i in range(strips - 1)])
    feats, w1, w2, coverage, shift = call(
        functools.partial(feature_kernel, optical=optical),
        "features",
        (
            shape((2, 4, layers, KDIM, half), BF16),
            shape((HIDDEN * 8, KDIM), BF16),
            shape((32, HIDDEN * 8), BF16),
            shape((8, half)),
            shape((32, 128)),
        ),
        [VMEM] * 2,
        volume,
        facts,
        scratch=[
            pltpu.VMEM((rows * columns // 128, 128), F32),
            pltpu.VMEM((layers, 8, 8, half), F32),
        ],
    )
    net = (w1, w2, coverage, shift)
    cores = [(i, i ^ 1) for i in range(depths)]
    sent = call(
        send_inner_kernel,
        "march_send_inner",
        shape((2, 4, 8, half)),
        [SMEM] + [VMEM] * 5,
        where,
        feats,
        *net,
    )
    inner = lax.ppermute(sent, "depth", cores)
    edges = call(
        edge_kernel,
        "edges",
        shape((2, layers, KDIM, half), BF16),
        [VMEM] * 3 + [pl.BlockSpec(memory_space=pl.ANY)],
        feats,
        top,
        bot,
        sent,
    )
    plane = pltpu.VMEM((layers, KDIM, half), BF16)
    sent = call(
        send_outer_kernel,
        "march_send_outer",
        shape((2, 4, 8, half)),
        [SMEM] + [VMEM] * 6,
        where,
        feats,
        edges,
        *net,
        scratch=[plane],
    )
    outer = lax.ppermute(sent, "depth", cores)
    parts = [None] * 4
    for step in (1, 2, 3, 0):
        piece = call(
            functools.partial(keep_kernel, step=step),
            f"march_keep{step}",
            shape((4, 8, half)),
            [SMEM, SMEM] + [VMEM] * 8,
            where,
            slab_order,
            feats,
            edges,
            *net,
            inner,
            outer,
            scratch=[plane],
        )
        if step:
            piece = lax.ppermute(piece, "depth", [(i, i ^ (step << 1)) for i in range(depths)])
        parts[step] = piece
    quads = call(
        merge_z_kernel,
        "merge_z",
        tuple(shape((4, 2, half)) for _ in range(4)),
        [SMEM, SMEM] + [VMEM] * 4,
        where,
        slab_order,
        *parts,
    )
    quads = [
        lax.ppermute(quads[k], "depth", [(i, i ^ (k << 3)) for i in range(depths)]) if k else quads[0]
        for k in range(4)
    ]
    picture = call(
        merge_x_kernel,
        "merge_x",
        shape((3, 2, half)),
        [SMEM, SMEM] + [VMEM] * 4,
        where,
        slab_order,
        *quads,
    )
    pairs = [(i, i + 1) for i in range(1, strips * depths - 1, 2)]
    apart = lax.ppermute(picture, ("strip", "depth"), pairs + [(j, i) for i, j in pairs])
    beside = lax.ppermute(picture, "depth", cores)
    filtered = call(
        filter_kernel,
        "filter",
        shape((3, 1, columns)),
        [SMEM] * 3 + [VMEM] * 3,
        where,
        conv_weight.reshape(-1),
        conv_bias,
        beside,
        picture,
        apart,
    )
    return filtered.reshape(3, 1, 1, 1, columns)


def solution(mesh):
    placed = (
        P("depth", "strip", None),
        P("depth", "strip", None),
        P(),
        P(),
        P(),
        P(),
        P(),
        P(),
        P(),
    )
    return jax.shard_map(
        shards,
        mesh=mesh,
        in_specs=placed,
        out_specs=P(None, "strip", None, "depth", None),
        check_vma=False,
    )
```

```python
import functools

import jax
import jax.numpy as jnp
from jax import lax
from jax.experimental import pallas as pl
from jax.experimental.pallas import tpu as pltpu
from jax.sharding import PartitionSpec as P

HIDDEN = 64
KDIM = 48
CHUNK = 512
LAG = 1
SPLIT = 2
FIRST = 2
ORDER = (2, 1, 3, 0)
F32 = jnp.float32
BF16 = jnp.bfloat16


def iota(shape, dim):
    return lax.broadcasted_iota(jnp.int32, shape, dim)


def prepare_weights(facts, w1, w2):
    bias = 0.5 * facts[4:5]
    hi = bias.astype(BF16).astype(F32)
    mid = (bias - hi).astype(BF16).astype(F32)
    low = bias - hi - mid
    table = jnp.concatenate(
        [0.5 * facts[0:4], hi, mid, low, jnp.zeros((1, HIDDEN), F32)], 0
    ).astype(BF16)
    spread = (iota((HIDDEN * 8, HIDDEN), 0) // 8 == iota((HIDDEN * 8, HIDDEN), 1)).astype(BF16)
    nt = (((1,), (1,)), ((), ()))
    by_row = lax.dot_general(spread, table, nt, preferred_element_type=F32).astype(BF16)
    slot = iota((8, KDIM), 0)
    col = iota((8, KDIM), 1)
    place = jnp.where(col < 32, col // 8, col - 28) == slot
    wide = jnp.dot(by_row, place.astype(BF16), preferred_element_type=F32)
    r = iota((HIDDEN * 8, KDIM), 0)
    k = iota((HIDDEN * 8, KDIM), 1)
    w1[...] = jnp.where((k >= 32) | (r % 8 == k % 8), wide, 0.0).astype(BF16)
    pick = (iota((32, 4), 0) // 8 == iota((32, 4), 1)).astype(BF16)
    out_rows = lax.dot_general(
        pick, facts[5:9].astype(BF16), (((1,), (0,)), ((), ())), preferred_element_type=F32
    ).astype(BF16)
    full = lax.dot_general(out_rows, spread, nt, preferred_element_type=F32)
    o = iota((32, HIDDEN * 8), 0)
    q = iota((32, HIDDEN * 8), 1)
    scale = jnp.where(o < 24, 0.5, 1.0)
    w2[...] = jnp.where(o % 8 == q % 8, full * scale, 0.0).astype(BF16)


def feature_kernel(
    vol, facts, feats, w1, w2, coverage, shift, lines, planes, *, optical
):
    layers, rows, columns = vol.shape
    half = columns // 2
    prepare_weights(facts, w1, w2)
    coverage[...] = coverage_of(facts[10:11], optical, half)
    for o in range(4):
        scale = 0.5 if o < 3 else 1.0
        shift[8 * o : 8 * o + 8] = jnp.broadcast_to(scale * facts[9:10, o : o + 1], (8, 128))
    blocks = half // 128

    def permute(z, carry):
        field = vol[z].astype(F32)
        for k in range(2 * blocks):
            lines[k * rows : (k + 1) * rows] = field[:, k * 128 : (k + 1) * 128]
        for j in range(8):
            for k in range(blocks):
                left = lines[pl.ds(k * rows + j, 4, stride=8)]
                right = lines[pl.ds((k + blocks) * rows + j, 4, stride=8)]
                planes[z, j, :, k * 128 : (k + 1) * 128] = jnp.concatenate([left, right], 0)
        return carry

    lax.fori_loop(0, layers, permute, 0)
    lane = iota((8, half), 1)
    sub = iota((8, half), 0)
    ones = jnp.ones((KDIM - 32, half), BF16)

    def gradients(z, carry):
        before = jnp.maximum(z - 1, 0)
        after = jnp.minimum(z + 1, layers - 1)
        for j in range(8):
            s = planes[z, j]
            ahead = pltpu.roll(s, half - 1, 1)
            behind = pltpu.roll(s, 1, 1)
            ahead = jnp.where(
                lane == half - 1, jnp.where(sub < 4, pltpu.roll(ahead, 4, 0), 0.0), ahead
            )
            behind = jnp.where(lane == 0, jnp.where(sub >= 4, pltpu.roll(behind, 4, 0), 0.0), behind)
            if j > 0:
                above = planes[z, j - 1]
            else:
                above = pltpu.roll(planes[z, 7], 1, 0)
            if j < 7:
                below = planes[z, j + 1]
            else:
                below = pltpu.roll(planes[z, 0], 7, 0)
            deep = planes[after, j] - planes[before, j]
            block = jnp.concatenate(
                [s, 0.5 * (ahead - behind), 0.5 * (below - above), 0.5 * deep], 0
            )
            feats[j % 2, j // 2, z, 0:32] = block.astype(BF16)
            feats[j % 2, j // 2, z, 32:KDIM] = ones
        return carry

    lax.fori_loop(0, layers, gradients, 0)


def edge_kernel(feats, top, bot, after, edges):
    layers = feats.shape[2]
    half = feats.shape[4]
    sub = iota((8, half), 0)

    def fix(z, carry):
        for parity, zpos, rim, low in ((0, 0, top, 0), (1, 3, bot, 3)):
            inner = feats[1 - parity, zpos, z, 0:16].astype(F32)[0:8]
            both = feats[parity, zpos, z, 16:32].astype(F32)
            line = rim[z].astype(F32)
            outer = jnp.where(sub < 4, line[:, :half], line[:, half:])
            slope = 0.5 * (inner - outer) if parity == 0 else 0.5 * (outer - inner)
            fixed = jnp.where(sub % 4 == low, slope, both[0:8])
            edges[parity, z, 0:16] = feats[parity, zpos, z, 0:16]
            edges[parity, z, 16:32] = jnp.concatenate([fixed, both[8:16]], 0).astype(BF16)
            edges[parity, z, 32:KDIM] = feats[parity, zpos, z, 32:KDIM]
        return carry

    lax.fori_loop(0, layers, fix, 0)


def load_plane(feats, edges, parity, zpos, x):
    at_edge = zpos == 3 * parity

    @pl.when(at_edge)
    def _():
        x[...] = edges[parity]

    @pl.when(jnp.logical_not(at_edge))
    def _():
        x[...] = feats[parity, zpos]


def march(plane, w1, w2, coverage, shift, out):
    layers, _, half = plane.shape
    lift = jnp.concatenate([shift[...]] * (CHUNK // 128), 1)
    steps = [(c, z) for c in range(0, half, CHUNK) for z in range(layers)]
    waiting = []
    states = {}
    part = HIDDEN * 8 // SPLIT
    for n in range(len(steps) + LAG):
        e = lift
        fresh = []
        for p in range(SPLIT):
            k = slice(p * part, (p + 1) * part)
            if n < len(steps):
                c, z = steps[n]
                u = jnp.dot(w1[k], plane[z, :, c : c + CHUNK], preferred_element_type=F32)
                fresh.append((u * jnp.tanh(u) + u).astype(BF16))
            if n >= LAG:
                e = e + jnp.dot(w2[:, k], waiting[n - LAG][p], preferred_element_type=F32)
        waiting.append(fresh)
        if n < LAG:
            continue
        c, z = steps[n - LAG]
        waiting[n - LAG] = None
        raw = e[24:32]
        density = jnp.maximum(raw, 0.0) + jnp.log1p(jnp.exp(-jnp.abs(raw)))
        alpha = 1.0 - jnp.exp(coverage[:, c : c + CHUNK] * density)
        colours = [0.5 * jnp.tanh(e[8 * o : 8 * o + 8]) + 0.5 for o in range(3)]
        if z == 0:
            state = [alpha * colour for colour in colours] + [1.0 - alpha]
        else:
            share = states[c][3] * alpha
            state = [states[c][o] + share * colours[o] for o in range(3)]
            state.append(states[c][3] * (1.0 - alpha))
        states[c] = state
        if z == layers - 1:
            for o in range(4):
                out[o, :, c : c + CHUNK] = states[c][o]


def coverage_of(occ, optical, half):
    blocks = half // 128
    sub = iota((8, 128), 0)
    scaled = -optical * occ
    cols = []
    for k in range(blocks):
        left = jnp.broadcast_to(scaled[:, k : k + 1], (8, 128))
        right = jnp.broadcast_to(scaled[:, k + blocks : k + blocks + 1], (8, 128))
        cols.append(jnp.where(sub < 4, left, right))
    return jnp.concatenate(cols, 1)


def send_inner_kernel(where, feats, w1, w2, coverage, shift, out):
    parity = 1 - (where[0] & 1)

    def piece(i, carry):
        march(feats.at[parity, 1 + i], w1, w2, coverage, shift, out.at[i])
        return carry

    lax.fori_loop(0, 2, piece, 0)


def send_outer_kernel(where, feats, edges, w1, w2, coverage, shift, out, x):
    parity = 1 - (where[0] & 1)

    def piece(i, carry):
        load_plane(feats, edges, parity, 3 * i, x)
        march(x, w1, w2, coverage, shift, out.at[i])
        return carry

    lax.fori_loop(0, 2, piece, 0)


def over(parts, places):
    colours = [None] * 3
    total = None
    for i, part in enumerate(parts):
        light = None
        for j, other in enumerate(parts):
            if j != i:
                factor = jnp.where(places[j] < places[i], other[3], 1.0)
                light = factor if light is None else light * factor
        for o in range(3):
            term = light * part[o]
            colours[o] = term if colours[o] is None else colours[o] + term
        total = part[3] if total is None else total * part[3]
    return (*colours, total)


def first_kernel(where, feats, edges, w1, w2, coverage, shift, out, x):
    d = where[0]
    load_plane(feats, edges, d & 1, ((d >> 1) & 3) ^ FIRST, x)
    march(x, w1, w2, coverage, shift, out)


def merge_cores(d, order, zpos, state, inner, outer):
    slot = zpos >> 1
    middle = (zpos == 1) | (zpos == 2)
    other = tuple(jnp.where(middle, inner[slot, o], outer[slot, o]) for o in range(4))
    return over((state, other), (order[d] & 1, order[d ^ 1] & 1))


def first_merge_kernel(where, order, raw, inner, outer, out):
    d = where[0]
    state = tuple(raw[o] for o in range(4))
    merged = merge_cores(d, order, ((d >> 1) & 3) ^ FIRST, state, inner, outer)
    for o in range(4):
        out[o] = merged[o]


def keep_kernel(
    where, order, feats, edges, w1, w2, coverage, shift, inner, outer, after, out, x, *, step
):
    d = where[0]
    zpos = ((d >> 1) & 3) ^ step
    load_plane(feats, edges, d & 1, zpos, x)
    march(x, w1, w2, coverage, shift, out)
    state = tuple(out[o] for o in range(4))
    merged = merge_cores(d, order, zpos, state, inner, outer)
    for o in range(4):
        out[o] = merged[o]


def merge_z_kernel(where, order, part0, part1, part2, part3, out):
    d = where[0]
    parts = [tuple(p[o] for o in range(4)) for p in (part0, part1, part2, part3)]
    places = [(order[d ^ (k << 1)] >> 1) & 3 for k in range(4)]
    merged = over(parts, places)
    odd = (d & 1) == 1
    for o in range(4):
        rows = [merged[o][k : k + 1] for k in range(8)]
        for t in range(4):
            before, after = (t - 1) % 4, (t + 1) % 4
            out[t, o] = jnp.concatenate(
                [
                    rows[t],
                    rows[4 + t],
                    jnp.where(odd, rows[before], rows[after]),
                    jnp.where(odd, rows[4 + before], rows[4 + after]),
                ],
                0,
            )


def merge_x_kernel(where, order, parts, centre, extra):
    d = where[0]
    group = [tuple(parts[k, o] for o in range(4)) for k in range(4)]
    places = [order[(d & 7) | (k << 3)] >> 3 for k in range(4)]
    merged = over(group, places)
    boundary = ((d & 7) == 0) | ((d & 7) == 7)
    for o in range(3):
        centre[o] = merged[o][0:2]
        extra[o] = jnp.where(boundary, merged[o][2:4], merged[o][0:2])


def filter_kernel(where, weight, bias, beside, centre, apart, out):
    half = centre.shape[2]
    even = (where[0] & 1) == 0
    lane = iota((2, half), 1)
    sub = iota((2, half), 0)
    sums = [jnp.full((2, half), bias[o], F32) for o in range(3)]
    for i in range(3):
        above = jnp.where(even, apart[i], beside[i])
        below = jnp.where(even, beside[i], apart[i])
        for a, row in enumerate((above, centre[i], below)):
            flipped = jnp.concatenate([row[1:2], row[0:1]], 0)
            left = jnp.where(
                lane == 0, jnp.where(sub == 1, pltpu.roll(flipped, 1, 1), 0.0), pltpu.roll(row, 1, 1)
            )
            right = jnp.where(
                lane == half - 1,
                jnp.where(sub == 0, pltpu.roll(flipped, half - 1, 1), 0.0),
                pltpu.roll(row, half - 1, 1),
            )
            for b, window in enumerate((left, row, right)):
                for o in range(3):
                    sums[o] = sums[o] + weight[((o * 3 + i) * 3 + a) * 3 + b] * window
    for o in range(3):
        out[o, :, :half] = sums[o][0:1]
        out[o, :, half:] = sums[o][1:2]


VMEM = pl.BlockSpec(memory_space=pltpu.VMEM)
SMEM = pl.BlockSpec(memory_space=pltpu.SMEM)


def call(kernel, name, outs, specs, *args, scratch=(), micros=1.0):
    return pl.pallas_call(
        kernel,
        out_shape=outs,
        in_specs=specs,
        out_specs=jax.tree.map(lambda _: VMEM, outs),
        scratch_shapes=scratch,
        compiler_params=pltpu.CompilerParams(vmem_limit_bytes=24 * 2**20),
        name=name,
        cost_estimate=pl.CostEstimate(
            flops=int(micros * 1e9), bytes_accessed=0, transcendentals=0
        ),
    )(*args)


def shape(dims, dtype=F32):
    return jax.ShapeDtypeStruct(dims, dtype)


def across_pairs(strips, depths):
    pairs = []
    for y in range(strips):
        for d in range(depths):
            x, low, target = d >> 3, d & 7, None
            if low == 7:
                target = (y, 8 * x) if x > 0 else (y + 1, 0)
            elif low == 0:
                target = (y, 8 * x + 7) if x < depths // 8 - 1 else (y - 1, d + 7)
            else:
                target = (y, d + 1 if d % 2 else d - 1)
            if 0 <= target[0] < strips:
                pairs.append((y * depths + d, target[0] * depths + target[1]))
    return pairs


def table_of(*arrays):
    flat = [v.reshape(-1, v.shape[-1]).astype(F32) for v in arrays]
    rows = sum(v.shape[0] for v in flat)
    total, at = 0.0, 0
    for v in flat:
        n, width = v.shape
        total = total + jnp.pad(v, ((at, rows - at - n), (0, HIDDEN - width)))
        at += n
    return total


def shards(volume, occupancy, slab_order, w_in, b_in, w_out, b_out, conv_weight, conv_bias):
    strips = lax.axis_size("strip")
    depths = lax.axis_size("depth")
    layers, rows, columns = volume.shape
    half = columns // 2
    optical = 2.0 / (layers * depths)
    d = lax.axis_index("depth")
    where = d.astype(jnp.int32).reshape(1)
    facts = table_of(w_in, b_in, w_out.T, b_out, occupancy)
    top = lax.ppermute(volume[:, rows - 1 :], "strip", [(i, i + 1) for i in range(strips - 1)])
    bot = lax.ppermute(volume[:, :1], "strip", [(i + 1, i) for i in range(strips - 1)])
    feats, w1, w2, coverage, shift = call(
        functools.partial(feature_kernel, optical=optical),
        "features",
        (
            shape((2, 4, layers, KDIM, half), BF16),
            shape((HIDDEN * 8, KDIM), BF16),
            shape((32, HIDDEN * 8), BF16),
            shape((8, half)),
            shape((32, 128)),
        ),
        [VMEM] * 2,
        volume,
        facts,
        scratch=[
            pltpu.VMEM((rows * columns // 128, 128), F32),
            pltpu.VMEM((layers, 8, 8, half), F32),
        ],
    )
    net = (w1, w2, coverage, shift)
    cores = [(i, i ^ 1) for i in range(depths)]
    sent = call(
        send_inner_kernel,
        "march_send_inner",
        shape((2, 4, 8, half)),
        [SMEM] + [VMEM] * 5,
        where,
        feats,
        *net,
        micros=6.7,
    )
    inner = lax.ppermute(sent, "depth", cores)
    edges = call(
        edge_kernel,
        "edges",
        shape((2, layers, KDIM, half), BF16),
        [VMEM] * 3 + [pl.BlockSpec(memory_space=pl.ANY)],
        feats,
        top,
        bot,
        sent,
    )
    plane = pltpu.VMEM((layers, KDIM, half), BF16)
    sent = call(
        send_outer_kernel,
        "march_send_outer",
        shape((2, 4, 8, half)),
        [SMEM] + [VMEM] * 6,
        where,
        feats,
        edges,
        *net,
        scratch=[plane],
        micros=6.8,
    )
    outer = lax.ppermute(sent, "depth", cores)
    raw = call(
        first_kernel,
        "march_first",
        shape((4, 8, half)),
        [SMEM] + [VMEM] * 6,
        where,
        feats,
        edges,
        *net,
        scratch=[plane],
        micros=4.0,
    )
    parts = [None] * 4
    for step in ORDER:
        if step == FIRST:
            piece = call(
                first_merge_kernel,
                "merge_first",
                shape((4, 8, half)),
                [SMEM, SMEM] + [VMEM] * 3,
                where,
                slab_order,
                raw,
                inner,
                outer,
            )
        else:
            piece = call(
                functools.partial(keep_kernel, step=step),
                f"march_keep{step}",
                shape((4, 8, half)),
                [SMEM, SMEM] + [VMEM] * 8 + [pl.BlockSpec(memory_space=pl.ANY)],
                where,
                slab_order,
                feats,
                edges,
                *net,
                inner,
                outer,
                earlier,
                scratch=[plane],
                micros=4.0,
            )
        earlier = piece
        if step:
            piece = lax.ppermute(piece, "depth", [(i, i ^ (step << 1)) for i in range(depths)])
        parts[step] = piece
    rows_out = call(
        merge_z_kernel,
        "merge_z",
        shape((4, 4, 4, half)),
        [SMEM, SMEM] + [VMEM] * 4,
        where,
        slab_order,
        *parts,
    )
    rows_in = lax.all_to_all(
        rows_out,
        "depth",
        0,
        0,
        tiled=True,
        axis_index_groups=[[i | (k << 3) for k in range(4)] for i in range(8)],
    )
    picture, extra = call(
        merge_x_kernel,
        "merge_x",
        (shape((3, 2, half)), shape((3, 2, half))),
        [SMEM, SMEM, VMEM],
        where,
        slab_order,
        rows_in,
    )
    apart = lax.ppermute(extra, ("strip", "depth"), across_pairs(strips, depths))
    beside = lax.ppermute(picture, "depth", cores)
    filtered = call(
        filter_kernel,
        "filter",
        shape((3, 1, columns)),
        [SMEM] * 3 + [VMEM] * 3,
        where,
        conv_weight.reshape(-1),
        conv_bias,
        beside,
        picture,
        apart,
    )
    return filtered.reshape(3, 1, 1, 1, columns)


def solution(mesh):
    placed = (
        P("depth", "strip", None),
        P("depth", "strip", None),
        P(),
        P(),
        P(),
        P(),
        P(),
        P(),
        P(),
    )
    return jax.shard_map(
        shards,
        mesh=mesh,
        in_specs=placed,
        out_specs=P(None, "strip", None, "depth", None),
        check_vma=False,
    )
```

```python
import functools

import jax
import jax.numpy as jnp
from jax import lax
from jax.experimental import pallas as pl
from jax.experimental.pallas import tpu as pltpu
from jax.sharding import PartitionSpec as P

HIDDEN = 64
KDIM = 48
CHUNK = 512
LAG = 1
SPLIT = 2
PLAN = (
    ("send", (2, 1)),
    ("send", (3,)),
    ("keep", (2, 1, 3)),
    ("send", (0,)),
    ("keep", (0,)),
)
AWAITED = (2,)
F32 = jnp.float32
BF16 = jnp.bfloat16


def iota(shape, dim):
    return lax.broadcasted_iota(jnp.int32, shape, dim)


def prepare_weights(facts, w1, w2):
    bias = 0.5 * facts[4:5]
    hi = bias.astype(BF16).astype(F32)
    mid = (bias - hi).astype(BF16).astype(F32)
    low = bias - hi - mid
    table = jnp.concatenate(
        [0.5 * facts[0:4], hi, mid, low, jnp.zeros((1, HIDDEN), F32)], 0
    ).astype(BF16)
    spread = (iota((HIDDEN * 8, HIDDEN), 0) // 8 == iota((HIDDEN * 8, HIDDEN), 1)).astype(BF16)
    nt = (((1,), (1,)), ((), ()))
    by_row = lax.dot_general(spread, table, nt, preferred_element_type=F32).astype(BF16)
    slot = iota((8, KDIM), 0)
    col = iota((8, KDIM), 1)
    place = jnp.where(col < 32, col // 8, col - 28) == slot
    wide = jnp.dot(by_row, place.astype(BF16), preferred_element_type=F32)
    r = iota((HIDDEN * 8, KDIM), 0)
    k = iota((HIDDEN * 8, KDIM), 1)
    w1[...] = jnp.where((k >= 32) | (r % 8 == k % 8), wide, 0.0).astype(BF16)
    pick = (iota((32, 4), 0) // 8 == iota((32, 4), 1)).astype(BF16)
    out_rows = lax.dot_general(
        pick, facts[5:9].astype(BF16), (((1,), (0,)), ((), ())), preferred_element_type=F32
    ).astype(BF16)
    full = lax.dot_general(out_rows, spread, nt, preferred_element_type=F32)
    o = iota((32, HIDDEN * 8), 0)
    q = iota((32, HIDDEN * 8), 1)
    scale = jnp.where(o < 24, 0.5, 1.0)
    w2[...] = jnp.where(o % 8 == q % 8, full * scale, 0.0).astype(BF16)


def feature_kernel(
    where, vol, facts, counts, feats, w1, w2, coverage, shift, flags, lines, planes, *, optical
):
    layers, rows, columns = vol.shape
    half = columns // 2
    prepare_weights(facts, w1, w2)
    coverage[...] = coverage_of(counts[0:1].astype(F32), optical, half)
    for o in range(4):
        scale = 0.5 if o < 3 else 1.0
        shift[8 * o : 8 * o + 8] = jnp.broadcast_to(scale * facts[9:10, o : o + 1], (8, 128))
    set_flags(flags, counts[1:2], where[0])
    blocks = half // 128

    def permute(z, carry):
        field = vol[z].astype(F32)
        for k in range(2 * blocks):
            lines[k * rows : (k + 1) * rows] = field[:, k * 128 : (k + 1) * 128]
        for j in range(8):
            for k in range(blocks):
                left = lines[pl.ds(k * rows + j, 4, stride=8)]
                right = lines[pl.ds((k + blocks) * rows + j, 4, stride=8)]
                planes[z, j, :, k * 128 : (k + 1) * 128] = jnp.concatenate([left, right], 0)
        return carry

    lax.fori_loop(0, layers, permute, 0)
    lane = iota((8, half), 1)
    sub = iota((8, half), 0)
    ones = jnp.ones((KDIM - 32, half), BF16)

    def gradients(z, carry):
        before = jnp.maximum(z - 1, 0)
        after = jnp.minimum(z + 1, layers - 1)
        for j in range(8):
            s = planes[z, j]
            ahead = pltpu.roll(s, half - 1, 1)
            behind = pltpu.roll(s, 1, 1)
            ahead = jnp.where(
                lane == half - 1, jnp.where(sub < 4, pltpu.roll(ahead, 4, 0), 0.0), ahead
            )
            behind = jnp.where(lane == 0, jnp.where(sub >= 4, pltpu.roll(behind, 4, 0), 0.0), behind)
            if j > 0:
                above = planes[z, j - 1]
            else:
                above = pltpu.roll(planes[z, 7], 1, 0)
            if j < 7:
                below = planes[z, j + 1]
            else:
                below = pltpu.roll(planes[z, 0], 7, 0)
            deep = planes[after, j] - planes[before, j]
            block = jnp.concatenate(
                [s, 0.5 * (ahead - behind), 0.5 * (below - above), 0.5 * deep], 0
            )
            feats[j % 2, j // 2, z, 0:32] = block.astype(BF16)
            feats[j % 2, j // 2, z, 32:KDIM] = ones
        return carry

    lax.fori_loop(0, layers, gradients, 0)


def edge_kernel(feats, top, bot, edges):
    layers = feats.shape[2]
    half = feats.shape[4]
    sub = iota((8, half), 0)

    def fix(z, carry):
        for parity, zpos, rim, low in ((0, 0, top, 0), (1, 3, bot, 3)):
            inner = feats[1 - parity, zpos, z, 0:16].astype(F32)[0:8]
            both = feats[parity, zpos, z, 16:32].astype(F32)
            line = rim[z].astype(F32)
            outer = jnp.where(sub < 4, line[:, :half], line[:, half:])
            slope = 0.5 * (inner - outer) if parity == 0 else 0.5 * (outer - inner)
            fixed = jnp.where(sub % 4 == low, slope, both[0:8])
            edges[parity, z, 0:16] = feats[parity, zpos, z, 0:16]
            edges[parity, z, 16:32] = jnp.concatenate([fixed, both[8:16]], 0).astype(BF16)
            edges[parity, z, 32:KDIM] = feats[parity, zpos, z, 32:KDIM]
        return carry

    lax.fori_loop(0, layers, fix, 0)


def load_plane(feats, edges, parity, zpos, x):
    at_edge = zpos == 3 * parity

    @pl.when(at_edge)
    def _():
        x[...] = edges[parity]

    @pl.when(jnp.logical_not(at_edge))
    def _():
        x[...] = feats[parity, zpos]


def march(plane, w1, w2, coverage, shift, out):
    layers, _, half = plane.shape
    lift = jnp.concatenate([shift[...]] * (CHUNK // 128), 1)
    steps = [(c, z) for c in range(0, half, CHUNK) for z in range(layers)]
    waiting = []
    states = {}
    part = HIDDEN * 8 // SPLIT
    for n in range(len(steps) + LAG):
        e = lift
        fresh = []
        for p in range(SPLIT):
            k = slice(p * part, (p + 1) * part)
            if n < len(steps):
                c, z = steps[n]
                u = jnp.dot(w1[k], plane[z, :, c : c + CHUNK], preferred_element_type=F32)
                fresh.append((u * jnp.tanh(u) + u).astype(BF16))
            if n >= LAG:
                e = e + jnp.dot(w2[:, k], waiting[n - LAG][p], preferred_element_type=F32)
        waiting.append(fresh)
        if n < LAG:
            continue
        c, z = steps[n - LAG]
        waiting[n - LAG] = None
        raw = e[24:32]
        density = jnp.maximum(raw, 0.0) + jnp.log1p(jnp.exp(-jnp.abs(raw)))
        alpha = 1.0 - jnp.exp(coverage[:, c : c + CHUNK] * density)
        colours = [0.5 * jnp.tanh(e[8 * o : 8 * o + 8]) + 0.5 for o in range(3)]
        if z == 0:
            state = [alpha * colour for colour in colours] + [1.0 - alpha]
        else:
            share = states[c][3] * alpha
            state = [states[c][o] + share * colours[o] for o in range(3)]
            state.append(states[c][3] * (1.0 - alpha))
        states[c] = state
        if z == layers - 1:
            for o in range(4):
                out[o, :, c : c + CHUNK] = states[c][o]


def coverage_of(occ, optical, half):
    blocks = half // 128
    sub = iota((8, 128), 0)
    scaled = -optical * occ
    cols = []
    for k in range(blocks):
        left = jnp.broadcast_to(scaled[:, k : k + 1], (8, 128))
        right = jnp.broadcast_to(scaled[:, k + blocks : k + blocks + 1], (8, 128))
        cols.append(jnp.where(sub < 4, left, right))
    return jnp.concatenate(cols, 1)


def send_kernel(where, feats, edges, w1, w2, coverage, shift, after, out, x, *, steps):
    d = where[0]
    parity = 1 - (d & 1)
    first, *others = steps

    def piece(i, carry):
        step = first
        for n, other in enumerate(others):
            step = jnp.where(i == n + 1, other, step)
        load_plane(feats, edges, parity, ((d >> 1) & 3) ^ step, x)
        march(x, w1, w2, coverage, shift, out.at[i])
        return carry

    lax.fori_loop(0, len(steps), piece, 0)


def over(parts, flags, base):
    rows, width = parts[0][3].shape
    front = {}
    n = base
    for i in range(len(parts)):
        for j in range(i + 1, len(parts)):
            flag = jnp.concatenate([flags[n, :rows]] * (width // 128), 1)
            front[i, j] = flag > 0.5
            n += 1
    colours = [None] * 3
    total = None
    for i, part in enumerate(parts):
        light = None
        for j, other in enumerate(parts):
            if j == i:
                continue
            if j < i:
                factor = jnp.where(front[j, i], other[3], 1.0)
            else:
                factor = jnp.where(front[i, j], 1.0, other[3])
            light = factor if light is None else light * factor
        for o in range(3):
            term = light * part[o]
            colours[o] = term if colours[o] is None else colours[o] + term
        total = part[3] if total is None else total * part[3]
    return (*colours, total)


def set_flags(flags, order, d):
    spot = iota((1, HIDDEN), 1)
    order = order.astype(F32)

    def place(index, bit, count):
        value = jnp.sum(jnp.where(spot == index, order, 0.0), axis=1, keepdims=True)
        return (value.astype(jnp.int32) >> bit) & (count - 1)

    groups = (
        [place(d ^ k, 0, 2) for k in range(2)],
        [place(d ^ (k << 1), 1, 4) for k in range(4)],
        [place((d & 7) | (k << 3), 3, 4) for k in range(4)],
    )
    n = 0
    for group in groups:
        for i in range(len(group)):
            for j in range(i + 1, len(group)):
                flag = jnp.where(group[i] < group[j], 1.0, 0.0)
                flags[n] = jnp.broadcast_to(flag, (8, 128))
                n += 1


def keep_kernel(
    where, flags, feats, edges, w1, w2, coverage, shift, received, *refs, step, slot
):
    out, x = refs[-2:]
    d = where[0]
    load_plane(feats, edges, d & 1, ((d >> 1) & 3) ^ step, x)
    march(x, w1, w2, coverage, shift, out)
    if step == 0:
        return
    state = tuple(out[o] for o in range(4))
    other = tuple(received[slot, o] for o in range(4))
    merged = over((state, other), flags, 0)
    for o in range(4):
        out[o] = merged[o]


def merge_z_kernel(where, flags, received, part0, part1, part2, part3, out):
    d = where[0]
    parts = [tuple(p[o] for o in range(4)) for p in (part0, part1, part2, part3)]
    parts[0] = over((parts[0], tuple(received[0, o] for o in range(4))), flags, 0)
    merged = over(parts, flags, 1)
    odd = (d & 1) == 1
    for o in range(4):
        rows = [merged[o][k : k + 1] for k in range(8)]
        for t in range(4):
            before, after = (t - 1) % 4, (t + 1) % 4
            out[t, o] = jnp.concatenate(
                [
                    rows[t],
                    rows[4 + t],
                    jnp.where(odd, rows[before], rows[after]),
                    jnp.where(odd, rows[4 + before], rows[4 + after]),
                ],
                0,
            )


def merge_x_kernel(where, flags, parts, centre, extra):
    d = where[0]
    group = [tuple(parts[k, o] for o in range(4)) for k in range(4)]
    merged = over(group, flags, 7)
    boundary = ((d & 7) == 0) | ((d & 7) == 7)
    for o in range(3):
        centre[o] = merged[o][0:2]
        extra[o] = jnp.where(boundary, merged[o][2:4], merged[o][0:2])


def filter_kernel(where, weight, bias, beside, centre, apart, out):
    half = centre.shape[2]
    even = (where[0] & 1) == 0
    lane = iota((2, half), 1)
    sub = iota((2, half), 0)
    spread = lambda v: jnp.concatenate([jnp.broadcast_to(v, (2, 128))] * (half // 128), 1)
    sums = [spread(bias[:, o : o + 1]) for o in range(3)]
    for i in range(3):
        above = jnp.where(even, apart[i], beside[i])
        below = jnp.where(even, beside[i], apart[i])
        for a, row in enumerate((above, centre[i], below)):
            flipped = jnp.concatenate([row[1:2], row[0:1]], 0)
            left = jnp.where(
                lane == 0, jnp.where(sub == 1, pltpu.roll(flipped, 1, 1), 0.0), pltpu.roll(row, 1, 1)
            )
            right = jnp.where(
                lane == half - 1,
                jnp.where(sub == 0, pltpu.roll(flipped, half - 1, 1), 0.0),
                pltpu.roll(row, half - 1, 1),
            )
            for b, window in enumerate((left, row, right)):
                for o in range(3):
                    sums[o] = sums[o] + spread(weight[o, i, a : a + 1, b : b + 1]) * window
    for o in range(3):
        out[o, :, :half] = sums[o][0:1]
        out[o, :, half:] = sums[o][1:2]


VMEM = pl.BlockSpec(memory_space=pltpu.VMEM)
SMEM = pl.BlockSpec(memory_space=pltpu.SMEM)
ANY = pl.BlockSpec(memory_space=pl.ANY)


def call(kernel, name, outs, specs, *args, scratch=(), micros=1.0):
    return pl.pallas_call(
        kernel,
        out_shape=outs,
        in_specs=specs,
        out_specs=jax.tree.map(lambda _: VMEM, outs),
        scratch_shapes=scratch,
        compiler_params=pltpu.CompilerParams(vmem_limit_bytes=24 * 2**20),
        name=name,
        cost_estimate=pl.CostEstimate(
            flops=int(micros * 1e9), bytes_accessed=0, transcendentals=0
        ),
    )(*args)


def shape(dims, dtype=F32):
    return jax.ShapeDtypeStruct(dims, dtype)


def across_pairs(strips, depths):
    pairs = []
    for y in range(strips):
        for d in range(depths):
            x, low, target = d >> 3, d & 7, None
            if low == 7:
                target = (y, 8 * x) if x > 0 else (y + 1, 0)
            elif low == 0:
                target = (y, 8 * x + 7) if x < depths // 8 - 1 else (y - 1, d + 7)
            else:
                target = (y, d + 1 if d % 2 else d - 1)
            if 0 <= target[0] < strips:
                pairs.append((y * depths + d, target[0] * depths + target[1]))
    return pairs


def table_of(kind, *arrays):
    flat = [v.reshape(-1, v.shape[-1]).astype(kind) for v in arrays]
    rows = sum(v.shape[0] for v in flat)
    total, at = jnp.zeros((rows, HIDDEN), kind), 0
    for v in flat:
        n, width = v.shape
        total = total + jnp.pad(v, ((at, rows - at - n), (0, HIDDEN - width)))
        at += n
    return total


def shards(volume, occupancy, slab_order, w_in, b_in, w_out, b_out, conv_weight, conv_bias):
    strips = lax.axis_size("strip")
    depths = lax.axis_size("depth")
    layers, rows, columns = volume.shape
    half = columns // 2
    optical = 2.0 / (layers * depths)
    d = lax.axis_index("depth")
    where = d.astype(jnp.int32).reshape(1)
    facts = table_of(F32, w_in, b_in, w_out.T, b_out)
    counts = table_of(jnp.int32, occupancy, slab_order)
    top = lax.ppermute(volume[:, rows - 1 :], "strip", [(i, i + 1) for i in range(strips - 1)])
    bot = lax.ppermute(volume[:, :1], "strip", [(i + 1, i) for i in range(strips - 1)])
    feats, w1, w2, coverage, shift, flags = call(
        functools.partial(feature_kernel, optical=optical),
        "features",
        (
            shape((2, 4, layers, KDIM, half), BF16),
            shape((HIDDEN * 8, KDIM), BF16),
            shape((32, HIDDEN * 8), BF16),
            shape((8, half)),
            shape((32, 128)),
            shape((13, 8, 128)),
        ),
        [SMEM] + [VMEM] * 3,
        where,
        volume,
        facts,
        counts,
        scratch=[
            pltpu.VMEM((rows * columns // 128, 128), F32),
            pltpu.VMEM((layers, 8, 8, half), F32),
        ],
    )
    net = (w1, w2, coverage, shift)
    cores = [(i, i ^ 1) for i in range(depths)]
    edges = call(
        edge_kernel,
        "edges",
        shape((2, layers, KDIM, half), BF16),
        [VMEM] * 3,
        feats,
        top,
        bot,
    )
    plane = pltpu.VMEM((layers, KDIM, half), BF16)
    latest = edges

    def send(steps):
        return call(
            functools.partial(send_kernel, steps=steps),
            "march_send" + "".join(map(str, steps)),
            shape((len(steps), 4, 8, half)),
            [SMEM] + [VMEM] * 6 + [ANY],
            where,
            feats,
            edges,
            *net,
            latest,
            scratch=[plane],
            micros=3.0 * len(steps),
        )

    def keep(step, received, slot, *landed):
        return call(
            functools.partial(keep_kernel, step=step, slot=slot),
            f"march_keep{step}",
            shape((4, 8, half)),
            [SMEM] + [VMEM] * 7 + [VMEM if step else ANY, ANY] + [ANY] * len(landed),
            where,
            flags,
            feats,
            edges,
            *net,
            received,
            latest,
            *landed,
            scratch=[plane],
            micros=3.0,
        )

    received, parts = {}, [None] * 4
    for kind, steps in PLAN:
        if kind == "send":
            latest = send(steps)
            arriving = lax.ppermute(latest, "depth", cores)
            for slot, step in enumerate(steps):
                received[step] = (arriving, slot)
            continue
        for step in steps:
            landed = [parts[n] for n in AWAITED] if step == 0 else []
            latest = keep(step, *received[step if step else 3], *landed)
            parts[step] = latest
            if step:
                swap = [(i, i ^ (step << 1)) for i in range(depths)]
                parts[step] = lax.ppermute(latest, "depth", swap)
    rows_out = call(
        merge_z_kernel,
        "merge_z",
        shape((4, 4, 4, half)),
        [SMEM] + [VMEM] * 6,
        where,
        flags,
        received[0][0],
        *parts,
    )
    rows_in = lax.all_to_all(
        rows_out,
        "depth",
        0,
        0,
        tiled=True,
        axis_index_groups=[[i | (k << 3) for k in range(4)] for i in range(8)],
    )
    picture, extra = call(
        merge_x_kernel,
        "merge_x",
        (shape((3, 2, half)), shape((3, 2, half))),
        [SMEM, VMEM, VMEM],
        where,
        flags,
        rows_in,
    )
    apart = lax.ppermute(extra, ("strip", "depth"), across_pairs(strips, depths))
    beside = lax.ppermute(picture, "depth", cores)
    filtered = call(
        filter_kernel,
        "filter",
        shape((3, 1, columns)),
        [SMEM] + [VMEM] * 5,
        where,
        conv_weight,
        conv_bias.reshape(1, 3),
        beside,
        picture,
        apart,
    )
    return filtered.reshape(3, 1, 1, 1, columns)


def solution(mesh):
    placed = (
        P("depth", "strip", None),
        P("depth", "strip", None),
        P(),
        P(),
        P(),
        P(),
        P(),
        P(),
        P(),
    )
    return jax.shard_map(
        shards,
        mesh=mesh,
        in_specs=placed,
        out_specs=P(None, "strip", None, "depth", None),
        check_vma=False,
    )
```

```python
import functools

import jax
import jax.numpy as jnp
from jax import lax
from jax.experimental import pallas as pl
from jax.experimental.pallas import tpu as pltpu
from jax.sharding import PartitionSpec as P

HIDDEN = 64
KDIM = 48
CHUNK = 512
LAG = 1
SPLIT = 2
PLAN = (
    ("send", (2, 1)),
    ("send", (3,)),
    ("keep", (2, 1, 3)),
    ("send", (0,)),
    ("keep", (0,)),
)
AWAITED = (2,)
F32 = jnp.float32
BF16 = jnp.bfloat16


def iota(shape, dim):
    return lax.broadcasted_iota(jnp.int32, shape, dim)


def prepare_weights(facts, w1, w2):
    bias = 0.5 * facts[4:5]
    hi = bias.astype(BF16).astype(F32)
    mid = (bias - hi).astype(BF16).astype(F32)
    low = bias - hi - mid
    table = jnp.concatenate(
        [0.5 * facts[0:4], hi, mid, low, jnp.zeros((1, HIDDEN), F32)], 0
    ).astype(BF16)
    spread = (iota((HIDDEN * 8, HIDDEN), 0) // 8 == iota((HIDDEN * 8, HIDDEN), 1)).astype(BF16)
    nt = (((1,), (1,)), ((), ()))
    by_row = lax.dot_general(spread, table, nt, preferred_element_type=F32).astype(BF16)
    slot = iota((8, KDIM), 0)
    col = iota((8, KDIM), 1)
    place = jnp.where(col < 32, col // 8, col - 28) == slot
    wide = jnp.dot(by_row, place.astype(BF16), preferred_element_type=F32)
    r = iota((HIDDEN * 8, KDIM), 0)
    k = iota((HIDDEN * 8, KDIM), 1)
    w1[...] = jnp.where((k >= 32) | (r % 8 == k % 8), wide, 0.0).astype(BF16)
    pick = (iota((32, 4), 0) // 8 == iota((32, 4), 1)).astype(BF16)
    out_rows = lax.dot_general(
        pick, facts[5:9].astype(BF16), (((1,), (0,)), ((), ())), preferred_element_type=F32
    ).astype(BF16)
    full = lax.dot_general(out_rows, spread, nt, preferred_element_type=F32)
    o = iota((32, HIDDEN * 8), 0)
    q = iota((32, HIDDEN * 8), 1)
    scale = jnp.where(o < 24, 0.5, 1.0)
    w2[...] = jnp.where(o % 8 == q % 8, full * scale, 0.0).astype(BF16)


def feature_kernel(
    where, vol, facts, counts, feats, w1, w2, coverage, shift, flags, lines, planes, *, optical
):
    layers, rows, columns = vol.shape
    half = columns // 2
    prepare_weights(facts, w1, w2)
    coverage[...] = coverage_of(counts[0:1].astype(F32), optical, half)
    for o in range(4):
        scale = 0.5 if o < 3 else 1.0
        shift[8 * o : 8 * o + 8] = jnp.broadcast_to(scale * facts[9:10, o : o + 1], (8, 128))
    set_flags(flags, counts[1:2], where[0])
    blocks = half // 128

    def permute(z, carry):
        field = vol[z].astype(F32)
        for k in range(2 * blocks):
            lines[k * rows : (k + 1) * rows] = field[:, k * 128 : (k + 1) * 128]
        for j in range(8):
            for k in range(blocks):
                left = lines[pl.ds(k * rows + j, 4, stride=8)]
                right = lines[pl.ds((k + blocks) * rows + j, 4, stride=8)]
                planes[z, j, :, k * 128 : (k + 1) * 128] = jnp.concatenate([left, right], 0)
        return carry

    lax.fori_loop(0, layers, permute, 0, unroll=4)
    lane = iota((8, half), 1)
    sub = iota((8, half), 0)
    ones = jnp.ones((KDIM - 32, half), BF16)

    def gradients(z, carry):
        before = jnp.maximum(z - 1, 0)
        after = jnp.minimum(z + 1, layers - 1)
        for j in range(8):
            s = planes[z, j]
            ahead = pltpu.roll(s, half - 1, 1)
            behind = pltpu.roll(s, 1, 1)
            ahead = jnp.where(
                lane == half - 1, jnp.where(sub < 4, pltpu.roll(ahead, 4, 0), 0.0), ahead
            )
            behind = jnp.where(lane == 0, jnp.where(sub >= 4, pltpu.roll(behind, 4, 0), 0.0), behind)
            if j > 0:
                above = planes[z, j - 1]
            else:
                above = pltpu.roll(planes[z, 7], 1, 0)
            if j < 7:
                below = planes[z, j + 1]
            else:
                below = pltpu.roll(planes[z, 0], 7, 0)
            deep = planes[after, j] - planes[before, j]
            block = jnp.concatenate(
                [s, 0.5 * (ahead - behind), 0.5 * (below - above), 0.5 * deep], 0
            )
            feats[j % 2, j // 2, z, 0:32] = block.astype(BF16)
            feats[j % 2, j // 2, z, 32:KDIM] = ones
        return carry

    lax.fori_loop(0, layers, gradients, 0, unroll=4)


def edge_kernel(feats, top, bot, edges):
    layers = feats.shape[2]
    half = feats.shape[4]
    sub = iota((8, half), 0)

    def fix(z, carry):
        for parity, zpos, rim, low in ((0, 0, top, 0), (1, 3, bot, 3)):
            inner = feats[1 - parity, zpos, z, 0:16].astype(F32)[0:8]
            both = feats[parity, zpos, z, 16:32].astype(F32)
            line = rim[z].astype(F32)
            outer = jnp.where(sub < 4, line[:, :half], line[:, half:])
            slope = 0.5 * (inner - outer) if parity == 0 else 0.5 * (outer - inner)
            fixed = jnp.where(sub % 4 == low, slope, both[0:8])
            edges[parity, z, 0:16] = feats[parity, zpos, z, 0:16]
            edges[parity, z, 16:32] = jnp.concatenate([fixed, both[8:16]], 0).astype(BF16)
            edges[parity, z, 32:KDIM] = feats[parity, zpos, z, 32:KDIM]
        return carry

    lax.fori_loop(0, layers, fix, 0)


def load_plane(feats, edges, parity, zpos, x):
    at_edge = zpos == 3 * parity

    @pl.when(at_edge)
    def _():
        x[...] = edges[parity]

    @pl.when(jnp.logical_not(at_edge))
    def _():
        x[...] = feats[parity, zpos]


def march(plane, w1, w2, coverage, shift, out):
    layers, _, half = plane.shape
    lift = jnp.concatenate([shift[...]] * (CHUNK // 128), 1)
    steps = [(c, z) for c in range(0, half, CHUNK) for z in range(layers)]
    waiting = []
    states = {}
    part = HIDDEN * 8 // SPLIT
    for n in range(len(steps) + LAG):
        e = lift
        fresh = []
        for p in range(SPLIT):
            k = slice(p * part, (p + 1) * part)
            if n < len(steps):
                c, z = steps[n]
                u = jnp.dot(w1[k], plane[z, :, c : c + CHUNK], preferred_element_type=F32)
                fresh.append((u * jnp.tanh(u) + u).astype(BF16))
            if n >= LAG:
                e = e + jnp.dot(w2[:, k], waiting[n - LAG][p], preferred_element_type=F32)
        waiting.append(fresh)
        if n < LAG:
            continue
        c, z = steps[n - LAG]
        waiting[n - LAG] = None
        raw = e[24:32]
        density = jnp.maximum(raw, 0.0) + jnp.log1p(jnp.exp(-jnp.abs(raw)))
        alpha = 1.0 - jnp.exp(coverage[:, c : c + CHUNK] * density)
        colours = [0.5 * jnp.tanh(e[8 * o : 8 * o + 8]) + 0.5 for o in range(3)]
        if z == 0:
            state = [alpha * colour for colour in colours] + [1.0 - alpha]
        else:
            share = states[c][3] * alpha
            state = [states[c][o] + share * colours[o] for o in range(3)]
            state.append(states[c][3] * (1.0 - alpha))
        states[c] = state
        if z == layers - 1:
            for o in range(4):
                out[o, :, c : c + CHUNK] = states[c][o]


def coverage_of(occ, optical, half):
    blocks = half // 128
    sub = iota((8, 128), 0)
    scaled = -optical * occ
    cols = []
    for k in range(blocks):
        left = jnp.broadcast_to(scaled[:, k : k + 1], (8, 128))
        right = jnp.broadcast_to(scaled[:, k + blocks : k + blocks + 1], (8, 128))
        cols.append(jnp.where(sub < 4, left, right))
    return jnp.concatenate(cols, 1)


def send_kernel(where, feats, edges, w1, w2, coverage, shift, after, out, x, *, steps):
    d = where[0]
    parity = 1 - (d & 1)
    first, *others = steps

    def piece(i, carry):
        step = first
        for n, other in enumerate(others):
            step = jnp.where(i == n + 1, other, step)
        load_plane(feats, edges, parity, ((d >> 1) & 3) ^ step, x)
        march(x, w1, w2, coverage, shift, out.at[i])
        return carry

    lax.fori_loop(0, len(steps), piece, 0)


def over(parts, flags, base):
    rows, width = parts[0][3].shape
    front = {}
    n = base
    for i in range(len(parts)):
        for j in range(i + 1, len(parts)):
            flag = jnp.concatenate([flags[n, :rows]] * (width // 128), 1)
            front[i, j] = flag > 0.5
            n += 1
    colours = [None] * 3
    total = None
    for i, part in enumerate(parts):
        light = None
        for j, other in enumerate(parts):
            if j == i:
                continue
            if j < i:
                factor = jnp.where(front[j, i], other[3], 1.0)
            else:
                factor = jnp.where(front[i, j], 1.0, other[3])
            light = factor if light is None else light * factor
        for o in range(3):
            term = light * part[o]
            colours[o] = term if colours[o] is None else colours[o] + term
        total = part[3] if total is None else total * part[3]
    return (*colours, total)


def set_flags(flags, order, d):
    spot = iota((1, HIDDEN), 1)
    order = order.astype(F32)

    def place(index, bit, count):
        value = jnp.sum(jnp.where(spot == index, order, 0.0), axis=1, keepdims=True)
        return (value.astype(jnp.int32) >> bit) & (count - 1)

    groups = (
        [place(d ^ k, 0, 2) for k in range(2)],
        [place(d ^ (k << 1), 1, 4) for k in range(4)],
        [place((d & 7) | (k << 3), 3, 4) for k in range(4)],
    )
    n = 0
    for group in groups:
        for i in range(len(group)):
            for j in range(i + 1, len(group)):
                flag = jnp.where(group[i] < group[j], 1.0, 0.0)
                flags[n] = jnp.broadcast_to(flag, (8, 128))
                n += 1


def keep_kernel(
    where, flags, feats, edges, w1, w2, coverage, shift, received, *refs, step, slot
):
    out, x = refs[-2:]
    d = where[0]
    load_plane(feats, edges, d & 1, ((d >> 1) & 3) ^ step, x)
    march(x, w1, w2, coverage, shift, out)
    if step == 0:
        return
    state = tuple(out[o] for o in range(4))
    other = tuple(received[slot, o] for o in range(4))
    merged = over((state, other), flags, 0)
    for o in range(4):
        out[o] = merged[o]


def merge_z_kernel(where, flags, received, part0, part1, part2, part3, out):
    d = where[0]
    parts = [tuple(p[o] for o in range(4)) for p in (part0, part1, part2, part3)]
    parts[0] = over((parts[0], tuple(received[0, o] for o in range(4))), flags, 0)
    merged = over(parts, flags, 1)
    odd = (d & 1) == 1
    for o in range(4):
        rows = [merged[o][k : k + 1] for k in range(8)]
        for t in range(4):
            before, after = (t - 1) % 4, (t + 1) % 4
            out[t, o] = jnp.concatenate(
                [
                    rows[t],
                    rows[4 + t],
                    jnp.where(odd, rows[before], rows[after]),
                    jnp.where(odd, rows[4 + before], rows[4 + after]),
                ],
                0,
            )


def merge_x_kernel(where, flags, parts, centre, extra):
    d = where[0]
    group = [tuple(parts[k, o] for o in range(4)) for k in range(4)]
    merged = over(group, flags, 7)
    boundary = ((d & 7) == 0) | ((d & 7) == 7)
    for o in range(3):
        centre[o] = merged[o][0:2]
        extra[o] = jnp.where(boundary, merged[o][2:4], merged[o][0:2])


def filter_kernel(where, weight, bias, beside, centre, apart, out):
    half = centre.shape[2]
    even = (where[0] & 1) == 0
    lane = iota((2, half), 1)
    sub = iota((2, half), 0)
    spread = lambda v: jnp.concatenate([jnp.broadcast_to(v, (2, 128))] * (half // 128), 1)
    sums = [spread(bias[:, o : o + 1]) for o in range(3)]
    for i in range(3):
        above = jnp.where(even, apart[i], beside[i])
        below = jnp.where(even, beside[i], apart[i])
        for a, row in enumerate((above, centre[i], below)):
            flipped = jnp.concatenate([row[1:2], row[0:1]], 0)
            left = jnp.where(
                lane == 0, jnp.where(sub == 1, pltpu.roll(flipped, 1, 1), 0.0), pltpu.roll(row, 1, 1)
            )
            right = jnp.where(
                lane == half - 1,
                jnp.where(sub == 0, pltpu.roll(flipped, half - 1, 1), 0.0),
                pltpu.roll(row, half - 1, 1),
            )
            for b, window in enumerate((left, row, right)):
                for o in range(3):
                    sums[o] = sums[o] + spread(weight[o, i, a : a + 1, b : b + 1]) * window
    for o in range(3):
        out[o, :, :half] = sums[o][0:1]
        out[o, :, half:] = sums[o][1:2]


VMEM = pl.BlockSpec(memory_space=pltpu.VMEM)
SMEM = pl.BlockSpec(memory_space=pltpu.SMEM)
ANY = pl.BlockSpec(memory_space=pl.ANY)


def call(kernel, name, outs, specs, *args, scratch=(), micros=1.0):
    return pl.pallas_call(
        kernel,
        out_shape=outs,
        in_specs=specs,
        out_specs=jax.tree.map(lambda _: VMEM, outs),
        scratch_shapes=scratch,
        compiler_params=pltpu.CompilerParams(vmem_limit_bytes=24 * 2**20),
        name=name,
        cost_estimate=pl.CostEstimate(
            flops=int(micros * 1e9), bytes_accessed=0, transcendentals=0
        ),
    )(*args)


def shape(dims, dtype=F32):
    return jax.ShapeDtypeStruct(dims, dtype)


def across_pairs(strips, depths):
    pairs = []
    for y in range(strips):
        for d in range(depths):
            x, low, target = d >> 3, d & 7, None
            if low == 7:
                target = (y, 8 * x) if x > 0 else (y + 1, 0)
            elif low == 0:
                target = (y, 8 * x + 7) if x < depths // 8 - 1 else (y - 1, d + 7)
            else:
                target = (y, d + 1 if d % 2 else d - 1)
            if 0 <= target[0] < strips:
                pairs.append((y * depths + d, target[0] * depths + target[1]))
    return pairs


def table_of(kind, *arrays):
    flat = [v.reshape(-1, v.shape[-1]).astype(kind) for v in arrays]
    rows = sum(v.shape[0] for v in flat)
    total, at = jnp.zeros((rows, HIDDEN), kind), 0
    for v in flat:
        n, width = v.shape
        total = total + jnp.pad(v, ((at, rows - at - n), (0, HIDDEN - width)))
        at += n
    return total


def shards(volume, occupancy, slab_order, w_in, b_in, w_out, b_out, conv_weight, conv_bias):
    strips = lax.axis_size("strip")
    depths = lax.axis_size("depth")
    layers, rows, columns = volume.shape
    half = columns // 2
    optical = 2.0 / (layers * depths)
    d = lax.axis_index("depth")
    where = d.astype(jnp.int32).reshape(1)
    facts = table_of(F32, w_in, b_in, w_out.T, b_out)
    counts = table_of(jnp.int32, occupancy, slab_order)
    top = lax.ppermute(volume[:, rows - 1 :], "strip", [(i, i + 1) for i in range(strips - 1)])
    bot = lax.ppermute(volume[:, :1], "strip", [(i + 1, i) for i in range(strips - 1)])
    feats, w1, w2, coverage, shift, flags = call(
        functools.partial(feature_kernel, optical=optical),
        "features",
        (
            shape((2, 4, layers, KDIM, half), BF16),
            shape((HIDDEN * 8, KDIM), BF16),
            shape((32, HIDDEN * 8), BF16),
            shape((8, half)),
            shape((32, 128)),
            shape((13, 8, 128)),
        ),
        [SMEM] + [VMEM] * 3,
        where,
        volume,
        facts,
        counts,
        scratch=[
            pltpu.VMEM((rows * columns // 128, 128), F32),
            pltpu.VMEM((layers, 8, 8, half), F32),
        ],
    )
    net = (w1, w2, coverage, shift)
    cores = [(i, i ^ 1) for i in range(depths)]
    edges = call(
        edge_kernel,
        "edges",
        shape((2, layers, KDIM, half), BF16),
        [VMEM] * 3,
        feats,
        top,
        bot,
    )
    plane = pltpu.VMEM((layers, KDIM, half), BF16)
    latest = edges

    def send(steps):
        return call(
            functools.partial(send_kernel, steps=steps),
            "march_send" + "".join(map(str, steps)),
            shape((len(steps), 4, 8, half)),
            [SMEM] + [VMEM] * 6 + [ANY],
            where,
            feats,
            edges,
            *net,
            latest,
            scratch=[plane],
            micros=3.0 * len(steps),
        )

    def keep(step, received, slot, *landed):
        return call(
            functools.partial(keep_kernel, step=step, slot=slot),
            f"march_keep{step}",
            shape((4, 8, half)),
            [SMEM] + [VMEM] * 7 + [VMEM if step else ANY, ANY] + [ANY] * len(landed),
            where,
            flags,
            feats,
            edges,
            *net,
            received,
            latest,
            *landed,
            scratch=[plane],
            micros=3.0,
        )

    received, parts = {}, [None] * 4
    for kind, steps in PLAN:
        if kind == "send":
            latest = send(steps)
            arriving = lax.ppermute(latest, "depth", cores)
            for slot, step in enumerate(steps):
                received[step] = (arriving, slot)
            continue
        for step in steps:
            landed = [parts[n] for n in AWAITED] if step == 0 else []
            latest = keep(step, *received[step if step else 3], *landed)
            parts[step] = latest
            if step:
                swap = [(i, i ^ (step << 1)) for i in range(depths)]
                parts[step] = lax.ppermute(latest, "depth", swap)
    rows_out = call(
        merge_z_kernel,
        "merge_z",
        shape((4, 4, 4, half)),
        [SMEM] + [VMEM] * 6,
        where,
        flags,
        received[0][0],
        *parts,
    )
    rows_in = lax.all_to_all(
        rows_out,
        "depth",
        0,
        0,
        tiled=True,
        axis_index_groups=[[i | (k << 3) for k in range(4)] for i in range(8)],
    )
    picture, extra = call(
        merge_x_kernel,
        "merge_x",
        (shape((3, 2, half)), shape((3, 2, half))),
        [SMEM, VMEM, VMEM],
        where,
        flags,
        rows_in,
    )
    apart = lax.ppermute(extra, ("strip", "depth"), across_pairs(strips, depths))
    beside = lax.ppermute(picture, "depth", cores)
    filtered = call(
        filter_kernel,
        "filter",
        shape((3, 1, columns)),
        [SMEM] + [VMEM] * 5,
        where,
        conv_weight,
        conv_bias.reshape(1, 3),
        beside,
        picture,
        apart,
    )
    return filtered.reshape(3, 1, 1, 1, columns)


def solution(mesh):
    placed = (
        P("depth", "strip", None),
        P("depth", "strip", None),
        P(),
        P(),
        P(),
        P(),
        P(),
        P(),
        P(),
    )
    return jax.shard_map(
        shards,
        mesh=mesh,
        in_specs=placed,
        out_specs=P(None, "strip", None, "depth", None),
        check_vma=False,
    )
```

```python
import functools

import jax
import jax.numpy as jnp
from jax import lax
from jax.experimental import pallas as pl
from jax.experimental.pallas import tpu as pltpu
from jax.sharding import PartitionSpec as P

HIDDEN = 64
KDIM = 48
CHUNK = 512
LAG = 1
SPLIT = 2
PLAN = (
    ("send", (2, 1)),
    ("send", (3,)),
    ("keep", (2, 1, 3)),
    ("send", (0,)),
    ("keep", (0,)),
)
AWAITED = (2,)
F32 = jnp.float32
BF16 = jnp.bfloat16


def iota(shape, dim):
    return lax.broadcasted_iota(jnp.int32, shape, dim)


def prepare_weights(facts, w1, w2):
    bias = 0.5 * facts[4:5]
    hi = bias.astype(BF16).astype(F32)
    mid = (bias - hi).astype(BF16).astype(F32)
    low = bias - hi - mid
    table = jnp.concatenate(
        [0.5 * facts[0:4], hi, mid, low, jnp.zeros((1, HIDDEN), F32)], 0
    ).astype(BF16)
    spread = (iota((HIDDEN * 8, HIDDEN), 0) // 8 == iota((HIDDEN * 8, HIDDEN), 1)).astype(BF16)
    nt = (((1,), (1,)), ((), ()))
    by_row = lax.dot_general(spread, table, nt, preferred_element_type=F32).astype(BF16)
    slot = iota((8, KDIM), 0)
    col = iota((8, KDIM), 1)
    place = jnp.where(col < 32, col // 8, col - 28) == slot
    wide = jnp.dot(by_row, place.astype(BF16), preferred_element_type=F32)
    r = iota((HIDDEN * 8, KDIM), 0)
    k = iota((HIDDEN * 8, KDIM), 1)
    w1[...] = jnp.where((k >= 32) | (r % 8 == k % 8), wide, 0.0).astype(BF16)
    pick = (iota((32, 4), 0) // 8 == iota((32, 4), 1)).astype(BF16)
    out_rows = lax.dot_general(
        pick, facts[5:9].astype(BF16), (((1,), (0,)), ((), ())), preferred_element_type=F32
    ).astype(BF16)
    full = lax.dot_general(out_rows, spread, nt, preferred_element_type=F32)
    o = iota((32, HIDDEN * 8), 0)
    q = iota((32, HIDDEN * 8), 1)
    scale = jnp.where(o < 24, 0.5, 1.0)
    w2[...] = jnp.where(o % 8 == q % 8, full * scale, 0.0).astype(BF16)


def feature_kernel(
    where, vol, facts, counts, feats, w1, w2, coverage, shift, flags, lines, planes, *, optical
):
    layers, rows, columns = vol.shape
    half = columns // 2
    prepare_weights(facts, w1, w2)
    coverage[...] = coverage_of(counts[0:1].astype(F32), optical, half)
    for o in range(4):
        scale = 0.5 if o < 3 else 1.0
        shift[8 * o : 8 * o + 8] = jnp.broadcast_to(scale * facts[9:10, o : o + 1], (8, 128))
    set_flags(flags, counts[1:2], where[0])
    blocks = half // 128

    def permute(z, carry):
        field = vol[z].astype(F32)
        for k in range(2 * blocks):
            lines[k * rows : (k + 1) * rows] = field[:, k * 128 : (k + 1) * 128]
        for j in range(8):
            for k in range(blocks):
                left = lines[pl.ds(k * rows + j, 4, stride=8)]
                right = lines[pl.ds((k + blocks) * rows + j, 4, stride=8)]
                planes[z, j, :, k * 128 : (k + 1) * 128] = jnp.concatenate([left, right], 0)
        return carry

    lax.fori_loop(0, layers, permute, 0, unroll=4)
    lane = iota((8, half), 1)
    sub = iota((8, half), 0)
    ones = jnp.ones((KDIM - 32, half), BF16)

    def gradients(z, carry):
        before = jnp.maximum(z - 1, 0)
        after = jnp.minimum(z + 1, layers - 1)
        for j in range(8):
            s = planes[z, j]
            ahead = pltpu.roll(s, half - 1, 1)
            behind = pltpu.roll(s, 1, 1)
            ahead = jnp.where(
                lane == half - 1, jnp.where(sub < 4, pltpu.roll(ahead, 4, 0), 0.0), ahead
            )
            behind = jnp.where(lane == 0, jnp.where(sub >= 4, pltpu.roll(behind, 4, 0), 0.0), behind)
            if j > 0:
                above = planes[z, j - 1]
            else:
                above = pltpu.roll(planes[z, 7], 1, 0)
            if j < 7:
                below = planes[z, j + 1]
            else:
                below = pltpu.roll(planes[z, 0], 7, 0)
            deep = planes[after, j] - planes[before, j]
            block = jnp.concatenate(
                [s, 0.5 * (ahead - behind), 0.5 * (below - above), 0.5 * deep], 0
            )
            feats[j % 2, j // 2, z, 0:32] = block.astype(BF16)
            feats[j % 2, j // 2, z, 32:KDIM] = ones
        return carry

    lax.fori_loop(0, layers, gradients, 0, unroll=4)


def edge_kernel(feats, top, bot, out):
    layers = feats.shape[2]
    half = feats.shape[4]
    sub = iota((8, half), 0)

    def fix(z, carry):
        for parity, zpos, rim, low in ((0, 0, top, 0), (1, 3, bot, 3)):
            inner = feats[1 - parity, zpos, z, 0:16].astype(F32)[0:8]
            both = feats[parity, zpos, z, 16:32].astype(F32)
            line = rim[z].astype(F32)
            outer = jnp.where(sub < 4, line[:, :half], line[:, half:])
            slope = 0.5 * (inner - outer) if parity == 0 else 0.5 * (outer - inner)
            fixed = jnp.where(sub % 4 == low, slope, both[0:8])
            fixed = jnp.concatenate([fixed, both[8:16]], 0).astype(BF16)
            out[parity, zpos, z, 16:32] = fixed
        return carry

    lax.fori_loop(0, layers, fix, 0)


def march(plane, w1, w2, coverage, shift, out):
    layers, _, half = plane.shape
    lift = jnp.concatenate([shift[...]] * (CHUNK // 128), 1)
    steps = [(c, z) for c in range(0, half, CHUNK) for z in range(layers)]
    waiting = []
    states = {}
    part = HIDDEN * 8 // SPLIT
    for n in range(len(steps) + LAG):
        e = lift
        fresh = []
        for p in range(SPLIT):
            k = slice(p * part, (p + 1) * part)
            if n < len(steps):
                c, z = steps[n]
                u = jnp.dot(w1[k], plane[z, :, c : c + CHUNK], preferred_element_type=F32)
                fresh.append((u * jnp.tanh(u) + u).astype(BF16))
            if n >= LAG:
                e = e + jnp.dot(w2[:, k], waiting[n - LAG][p], preferred_element_type=F32)
        waiting.append(fresh)
        if n < LAG:
            continue
        c, z = steps[n - LAG]
        waiting[n - LAG] = None
        raw = e[24:32]
        density = jnp.maximum(raw, 0.0) + jnp.log1p(jnp.exp(-jnp.abs(raw)))
        alpha = 1.0 - jnp.exp(coverage[:, c : c + CHUNK] * density)
        colours = [0.5 * jnp.tanh(e[8 * o : 8 * o + 8]) + 0.5 for o in range(3)]
        if z == 0:
            state = [alpha * colour for colour in colours] + [1.0 - alpha]
        else:
            share = states[c][3] * alpha
            state = [states[c][o] + share * colours[o] for o in range(3)]
            state.append(states[c][3] * (1.0 - alpha))
        states[c] = state
        if z == layers - 1:
            for o in range(4):
                out[o, :, c : c + CHUNK] = states[c][o]


def coverage_of(occ, optical, half):
    blocks = half // 128
    sub = iota((8, 128), 0)
    scaled = -optical * occ
    cols = []
    for k in range(blocks):
        left = jnp.broadcast_to(scaled[:, k : k + 1], (8, 128))
        right = jnp.broadcast_to(scaled[:, k + blocks : k + blocks + 1], (8, 128))
        cols.append(jnp.where(sub < 4, left, right))
    return jnp.concatenate(cols, 1)


def send_kernel(where, feats, w1, w2, coverage, shift, after, out, *, steps):
    d = where[0]
    parity = 1 - (d & 1)
    first, *others = steps

    def piece(i, carry):
        step = first
        for n, other in enumerate(others):
            step = jnp.where(i == n + 1, other, step)
        march(feats.at[parity, ((d >> 1) & 3) ^ step], w1, w2, coverage, shift, out.at[i])
        return carry

    lax.fori_loop(0, len(steps), piece, 0)


def over(parts, flags, base):
    rows, width = parts[0][3].shape
    front = {}
    n = base
    for i in range(len(parts)):
        for j in range(i + 1, len(parts)):
            flag = jnp.concatenate([flags[n, :rows]] * (width // 128), 1)
            front[i, j] = flag > 0.5
            n += 1
    colours = [None] * 3
    total = None
    for i, part in enumerate(parts):
        light = None
        for j, other in enumerate(parts):
            if j == i:
                continue
            if j < i:
                factor = jnp.where(front[j, i], other[3], 1.0)
            else:
                factor = jnp.where(front[i, j], 1.0, other[3])
            light = factor if light is None else light * factor
        for o in range(3):
            term = light * part[o]
            colours[o] = term if colours[o] is None else colours[o] + term
        total = part[3] if total is None else total * part[3]
    return (*colours, total)


def set_flags(flags, order, d):
    spot = iota((1, HIDDEN), 1)
    order = order.astype(F32)

    def place(index, bit, count):
        value = jnp.sum(jnp.where(spot == index, order, 0.0), axis=1, keepdims=True)
        return (value.astype(jnp.int32) >> bit) & (count - 1)

    groups = (
        [place(d ^ k, 0, 2) for k in range(2)],
        [place(d ^ (k << 1), 1, 4) for k in range(4)],
        [place((d & 7) | (k << 3), 3, 4) for k in range(4)],
    )
    n = 0
    for group in groups:
        for i in range(len(group)):
            for j in range(i + 1, len(group)):
                flag = jnp.where(group[i] < group[j], 1.0, 0.0)
                flags[n] = jnp.broadcast_to(flag, (8, 128))
                n += 1


def keep_kernel(
    where, flags, feats, w1, w2, coverage, shift, received, *refs, step, slot
):
    out = refs[-1]
    d = where[0]
    march(feats.at[d & 1, ((d >> 1) & 3) ^ step], w1, w2, coverage, shift, out)
    if step == 0:
        return
    state = tuple(out[o] for o in range(4))
    other = tuple(received[slot, o] for o in range(4))
    merged = over((state, other), flags, 0)
    for o in range(4):
        out[o] = merged[o]


def merge_z_kernel(where, flags, received, part0, part1, part2, part3, out):
    d = where[0]
    parts = [tuple(p[o] for o in range(4)) for p in (part0, part1, part2, part3)]
    parts[0] = over((parts[0], tuple(received[0, o] for o in range(4))), flags, 0)
    merged = over(parts, flags, 1)
    odd = (d & 1) == 1
    for o in range(4):
        rows = [merged[o][k : k + 1] for k in range(8)]
        for t in range(4):
            before, after = (t - 1) % 4, (t + 1) % 4
            out[t, o] = jnp.concatenate(
                [
                    rows[t],
                    rows[4 + t],
                    jnp.where(odd, rows[before], rows[after]),
                    jnp.where(odd, rows[4 + before], rows[4 + after]),
                ],
                0,
            )


def merge_x_kernel(where, flags, parts, centre, extra):
    d = where[0]
    group = [tuple(parts[k, o] for o in range(4)) for k in range(4)]
    merged = over(group, flags, 7)
    boundary = ((d & 7) == 0) | ((d & 7) == 7)
    for o in range(3):
        centre[o] = merged[o][0:2]
        extra[o] = jnp.where(boundary, merged[o][2:4], merged[o][0:2])


def filter_kernel(where, weight, bias, beside, centre, apart, out):
    half = centre.shape[2]
    even = (where[0] & 1) == 0
    lane = iota((2, half), 1)
    sub = iota((2, half), 0)
    spread = lambda v: jnp.concatenate([jnp.broadcast_to(v, (2, 128))] * (half // 128), 1)
    sums = [spread(bias[:, o : o + 1]) for o in range(3)]
    for i in range(3):
        above = jnp.where(even, apart[i], beside[i])
        below = jnp.where(even, beside[i], apart[i])
        for a, row in enumerate((above, centre[i], below)):
            flipped = jnp.concatenate([row[1:2], row[0:1]], 0)
            left = jnp.where(
                lane == 0, jnp.where(sub == 1, pltpu.roll(flipped, 1, 1), 0.0), pltpu.roll(row, 1, 1)
            )
            right = jnp.where(
                lane == half - 1,
                jnp.where(sub == 0, pltpu.roll(flipped, half - 1, 1), 0.0),
                pltpu.roll(row, half - 1, 1),
            )
            for b, window in enumerate((left, row, right)):
                for o in range(3):
                    sums[o] = sums[o] + spread(weight[o, i, a : a + 1, b : b + 1]) * window
    for o in range(3):
        out[o, :, :half] = sums[o][0:1]
        out[o, :, half:] = sums[o][1:2]


VMEM = pl.BlockSpec(memory_space=pltpu.VMEM)
SMEM = pl.BlockSpec(memory_space=pltpu.SMEM)
ANY = pl.BlockSpec(memory_space=pl.ANY)


def call(kernel, name, outs, specs, *args, scratch=(), micros=1.0, aliases={}):
    return pl.pallas_call(
        kernel,
        out_shape=outs,
        in_specs=specs,
        out_specs=jax.tree.map(lambda _: VMEM, outs),
        scratch_shapes=scratch,
        input_output_aliases=aliases,
        compiler_params=pltpu.CompilerParams(vmem_limit_bytes=24 * 2**20),
        name=name,
        cost_estimate=pl.CostEstimate(
            flops=int(micros * 1e9), bytes_accessed=0, transcendentals=0
        ),
    )(*args)


def shape(dims, dtype=F32):
    return jax.ShapeDtypeStruct(dims, dtype)


def across_pairs(strips, depths):
    pairs = []
    for y in range(strips):
        for d in range(depths):
            x, low, target = d >> 3, d & 7, None
            if low == 7:
                target = (y, 8 * x) if x > 0 else (y + 1, 0)
            elif low == 0:
                target = (y, 8 * x + 7) if x < depths // 8 - 1 else (y - 1, d + 7)
            else:
                target = (y, d + 1 if d % 2 else d - 1)
            if 0 <= target[0] < strips:
                pairs.append((y * depths + d, target[0] * depths + target[1]))
    return pairs


def table_of(kind, *arrays):
    flat = [v.reshape(-1, v.shape[-1]).astype(kind) for v in arrays]
    rows = sum(v.shape[0] for v in flat)
    total, at = jnp.zeros((rows, HIDDEN), kind), 0
    for v in flat:
        n, width = v.shape
        total = total + jnp.pad(v, ((at, rows - at - n), (0, HIDDEN - width)))
        at += n
    return total


def shards(volume, occupancy, slab_order, w_in, b_in, w_out, b_out, conv_weight, conv_bias):
    strips = lax.axis_size("strip")
    depths = lax.axis_size("depth")
    layers, rows, columns = volume.shape
    half = columns // 2
    optical = 2.0 / (layers * depths)
    d = lax.axis_index("depth")
    where = d.astype(jnp.int32).reshape(1)
    facts = table_of(F32, w_in, b_in, w_out.T, b_out)
    counts = table_of(jnp.int32, occupancy, slab_order)
    top = lax.ppermute(volume[:, rows - 1 :], "strip", [(i, i + 1) for i in range(strips - 1)])
    bot = lax.ppermute(volume[:, :1], "strip", [(i + 1, i) for i in range(strips - 1)])
    feats, w1, w2, coverage, shift, flags = call(
        functools.partial(feature_kernel, optical=optical),
        "features",
        (
            shape((2, 4, layers, KDIM, half), BF16),
            shape((HIDDEN * 8, KDIM), BF16),
            shape((32, HIDDEN * 8), BF16),
            shape((8, half)),
            shape((32, 128)),
            shape((13, 8, 128)),
        ),
        [SMEM] + [VMEM] * 3,
        where,
        volume,
        facts,
        counts,
        scratch=[
            pltpu.VMEM((rows * columns // 128, 128), F32),
            pltpu.VMEM((layers, 8, 8, half), F32),
        ],
    )
    net = (w1, w2, coverage, shift)
    cores = [(i, i ^ 1) for i in range(depths)]
    feats = call(
        edge_kernel,
        "edges",
        shape(feats.shape, BF16),
        [VMEM] * 3,
        feats,
        top,
        bot,
        aliases={0: 0},
    )
    latest = shift

    def send(steps):
        return call(
            functools.partial(send_kernel, steps=steps),
            "march_send" + "".join(map(str, steps)),
            shape((len(steps), 4, 8, half)),
            [SMEM] + [VMEM] * 5 + [ANY],
            where,
            feats,
            *net,
            latest,
            micros=3.0 * len(steps),
        )

    def keep(step, received, slot, *landed):
        return call(
            functools.partial(keep_kernel, step=step, slot=slot),
            f"march_keep{step}",
            shape((4, 8, half)),
            [SMEM] + [VMEM] * 6 + [VMEM if step else ANY, ANY] + [ANY] * len(landed),
            where,
            flags,
            feats,
            *net,
            received,
            latest,
            *landed,
            micros=3.0,
        )

    received, parts = {}, [None] * 4
    for kind, steps in PLAN:
        if kind == "send":
            latest = send(steps)
            arriving = lax.ppermute(latest, "depth", cores)
            for slot, step in enumerate(steps):
                received[step] = (arriving, slot)
            continue
        for step in steps:
            landed = [parts[n] for n in AWAITED] if step == 0 else []
            latest = keep(step, *received[step if step else 3], *landed)
            parts[step] = latest
            if step:
                swap = [(i, i ^ (step << 1)) for i in range(depths)]
                parts[step] = lax.ppermute(latest, "depth", swap)
    rows_out = call(
        merge_z_kernel,
        "merge_z",
        shape((4, 4, 4, half)),
        [SMEM] + [VMEM] * 6,
        where,
        flags,
        received[0][0],
        *parts,
    )
    rows_in = lax.all_to_all(
        rows_out,
        "depth",
        0,
        0,
        tiled=True,
        axis_index_groups=[[i | (k << 3) for k in range(4)] for i in range(8)],
    )
    picture, extra = call(
        merge_x_kernel,
        "merge_x",
        (shape((3, 2, half)), shape((3, 2, half))),
        [SMEM, VMEM, VMEM],
        where,
        flags,
        rows_in,
    )
    apart = lax.ppermute(extra, ("strip", "depth"), across_pairs(strips, depths))
    beside = lax.ppermute(picture, "depth", cores)
    filtered = call(
        filter_kernel,
        "filter",
        shape((3, 1, columns)),
        [SMEM] + [VMEM] * 5,
        where,
        conv_weight,
        conv_bias.reshape(1, 3),
        beside,
        picture,
        apart,
    )
    return filtered.reshape(3, 1, 1, 1, columns)


def solution(mesh):
    placed = (
        P("depth", "strip", None),
        P("depth", "strip", None),
        P(),
        P(),
        P(),
        P(),
        P(),
        P(),
        P(),
    )
    return jax.shard_map(
        shards,
        mesh=mesh,
        in_specs=placed,
        out_specs=P(None, "strip", None, "depth", None),
        check_vma=False,
    )
```

```python
import functools

import jax
import jax.numpy as jnp
from jax import lax
from jax.experimental import pallas as pl
from jax.experimental.pallas import tpu as pltpu
from jax.sharding import PartitionSpec as P

HIDDEN = 64
KDIM = 48
CHUNK = 512
LAG = 1
SPLIT = 2
PLAN = (
    ("send", (2, 1)),
    ("send", (3,)),
    ("keep", (2, 1, 3)),
    ("send", (0,)),
    ("keep", (0,)),
)
AWAITED = (2,)
F32 = jnp.float32
BF16 = jnp.bfloat16


def iota(shape, dim):
    return lax.broadcasted_iota(jnp.int32, shape, dim)


def prepare_weights(facts, w1, w2):
    bias = 0.5 * facts[4:5]
    hi = bias.astype(BF16).astype(F32)
    mid = (bias - hi).astype(BF16).astype(F32)
    low = bias - hi - mid
    table = jnp.concatenate(
        [0.5 * facts[0:4], hi, mid, low, jnp.zeros((1, HIDDEN), F32)], 0
    ).astype(BF16)
    spread = (iota((HIDDEN * 8, HIDDEN), 0) // 8 == iota((HIDDEN * 8, HIDDEN), 1)).astype(BF16)
    nt = (((1,), (1,)), ((), ()))
    by_row = lax.dot_general(spread, table, nt, preferred_element_type=F32).astype(BF16)
    slot = iota((8, KDIM), 0)
    col = iota((8, KDIM), 1)
    place = jnp.where(col < 32, col // 8, col - 28) == slot
    wide = jnp.dot(by_row, place.astype(BF16), preferred_element_type=F32)
    r = iota((HIDDEN * 8, KDIM), 0)
    k = iota((HIDDEN * 8, KDIM), 1)
    w1[...] = jnp.where((k >= 32) | (r % 8 == k % 8), wide, 0.0).astype(BF16)
    pick = (iota((32, 4), 0) // 8 == iota((32, 4), 1)).astype(BF16)
    out_rows = lax.dot_general(
        pick, facts[5:9].astype(BF16), (((1,), (0,)), ((), ())), preferred_element_type=F32
    ).astype(BF16)
    full = lax.dot_general(out_rows, spread, nt, preferred_element_type=F32)
    o = iota((32, HIDDEN * 8), 0)
    q = iota((32, HIDDEN * 8), 1)
    scale = jnp.where(o < 24, 0.5, 1.0)
    w2[...] = jnp.where(o % 8 == q % 8, full * scale, 0.0).astype(BF16)


def feature_kernel(
    where, vol, facts, counts, feats, w1, w2, coverage, shift, flags, lines, planes, *, optical
):
    layers, rows, columns = vol.shape
    half = columns // 2
    prepare_weights(facts, w1, w2)
    coverage[...] = coverage_of(counts[0:1].astype(F32), optical, half)
    for o in range(4):
        scale = 0.5 if o < 3 else 1.0
        shift[8 * o : 8 * o + 8] = jnp.broadcast_to(scale * facts[9:10, o : o + 1], (8, 128))
    set_flags(flags, counts[1:2], where[0])
    blocks = half // 128

    def permute(z, carry):
        field = vol[z].astype(F32)
        for k in range(2 * blocks):
            lines[k * rows : (k + 1) * rows] = field[:, k * 128 : (k + 1) * 128]
        for j in range(8):
            for k in range(blocks):
                left = lines[pl.ds(k * rows + j, 4, stride=8)]
                right = lines[pl.ds((k + blocks) * rows + j, 4, stride=8)]
                planes[z, j, :, k * 128 : (k + 1) * 128] = jnp.concatenate([left, right], 0)
        return carry

    lax.fori_loop(0, layers, permute, 0, unroll=8)
    lane = iota((8, half), 1)
    sub = iota((8, half), 0)
    ones = jnp.ones((KDIM - 32, half), BF16)

    def gradients(z, carry):
        before = jnp.maximum(z - 1, 0)
        after = jnp.minimum(z + 1, layers - 1)
        for j in range(8):
            s = planes[z, j]
            ahead = pltpu.roll(s, half - 1, 1)
            behind = pltpu.roll(s, 1, 1)
            ahead = jnp.where(
                lane == half - 1, jnp.where(sub < 4, pltpu.roll(ahead, 4, 0), 0.0), ahead
            )
            behind = jnp.where(lane == 0, jnp.where(sub >= 4, pltpu.roll(behind, 4, 0), 0.0), behind)
            if j > 0:
                above = planes[z, j - 1]
            else:
                above = pltpu.roll(planes[z, 7], 1, 0)
            if j < 7:
                below = planes[z, j + 1]
            else:
                below = pltpu.roll(planes[z, 0], 7, 0)
            deep = planes[after, j] - planes[before, j]
            block = jnp.concatenate(
                [s, 0.5 * (ahead - behind), 0.5 * (below - above), 0.5 * deep], 0
            )
            feats[j % 2, j // 2, z, 0:32] = block.astype(BF16)
            feats[j % 2, j // 2, z, 32:KDIM] = ones
        return carry

    lax.fori_loop(0, layers, gradients, 0, unroll=8)


def edge_kernel(feats, top, bot, out):
    layers = feats.shape[2]
    half = feats.shape[4]
    sub = iota((8, half), 0)

    def fix(z, carry):
        for parity, zpos, rim, low in ((0, 0, top, 0), (1, 3, bot, 3)):
            inner = feats[1 - parity, zpos, z, 0:16].astype(F32)[0:8]
            both = feats[parity, zpos, z, 16:32].astype(F32)
            line = rim[z].astype(F32)
            outer = jnp.where(sub < 4, line[:, :half], line[:, half:])
            slope = 0.5 * (inner - outer) if parity == 0 else 0.5 * (outer - inner)
            fixed = jnp.where(sub % 4 == low, slope, both[0:8])
            fixed = jnp.concatenate([fixed, both[8:16]], 0).astype(BF16)
            out[parity, zpos, z, 16:32] = fixed
        return carry

    lax.fori_loop(0, layers, fix, 0)


def march(plane, w1, w2, coverage, shift, out):
    layers, _, half = plane.shape
    lift = jnp.concatenate([shift[...]] * (CHUNK // 128), 1)
    steps = [(c, z) for c in range(0, half, CHUNK) for z in range(layers)]
    waiting = []
    states = {}
    part = HIDDEN * 8 // SPLIT
    for n in range(len(steps) + LAG):
        e = lift
        fresh = []
        for p in range(SPLIT):
            k = slice(p * part, (p + 1) * part)
            if n < len(steps):
                c, z = steps[n]
                u = jnp.dot(w1[k], plane[z, :, c : c + CHUNK], preferred_element_type=F32)
                fresh.append((u * jnp.tanh(u) + u).astype(BF16))
            if n >= LAG:
                e = e + jnp.dot(w2[:, k], waiting[n - LAG][p], preferred_element_type=F32)
        waiting.append(fresh)
        if n < LAG:
            continue
        c, z = steps[n - LAG]
        waiting[n - LAG] = None
        raw = e[24:32]
        density = jnp.maximum(raw, 0.0) + jnp.log1p(jnp.exp(-jnp.abs(raw)))
        alpha = 1.0 - jnp.exp(coverage[:, c : c + CHUNK] * density)
        colours = [0.5 * jnp.tanh(e[8 * o : 8 * o + 8]) + 0.5 for o in range(3)]
        if z == 0:
            state = [alpha * colour for colour in colours] + [1.0 - alpha]
        else:
            share = states[c][3] * alpha
            state = [states[c][o] + share * colours[o] for o in range(3)]
            state.append(states[c][3] * (1.0 - alpha))
        states[c] = state
        if z == layers - 1:
            for o in range(4):
                out[o, :, c : c + CHUNK] = states[c][o]


def coverage_of(occ, optical, half):
    blocks = half // 128
    sub = iota((8, 128), 0)
    scaled = -optical * occ
    cols = []
    for k in range(blocks):
        left = jnp.broadcast_to(scaled[:, k : k + 1], (8, 128))
        right = jnp.broadcast_to(scaled[:, k + blocks : k + blocks + 1], (8, 128))
        cols.append(jnp.where(sub < 4, left, right))
    return jnp.concatenate(cols, 1)


def send_kernel(where, feats, w1, w2, coverage, shift, after, out, *, steps):
    d = where[0]
    parity = 1 - (d & 1)
    first, *others = steps

    def piece(i, carry):
        step = first
        for n, other in enumerate(others):
            step = jnp.where(i == n + 1, other, step)
        march(feats.at[parity, ((d >> 1) & 3) ^ step], w1, w2, coverage, shift, out.at[i])
        return carry

    lax.fori_loop(0, len(steps), piece, 0)


def over(parts, flags, base):
    rows, width = parts[0][3].shape
    front = {}
    n = base
    for i in range(len(parts)):
        for j in range(i + 1, len(parts)):
            flag = jnp.concatenate([flags[n, :rows]] * (width // 128), 1)
            front[i, j] = flag > 0.5
            n += 1
    colours = [None] * 3
    total = None
    for i, part in enumerate(parts):
        light = None
        for j, other in enumerate(parts):
            if j == i:
                continue
            if j < i:
                factor = jnp.where(front[j, i], other[3], 1.0)
            else:
                factor = jnp.where(front[i, j], 1.0, other[3])
            light = factor if light is None else light * factor
        for o in range(3):
            term = light * part[o]
            colours[o] = term if colours[o] is None else colours[o] + term
        total = part[3] if total is None else total * part[3]
    return (*colours, total)


def set_flags(flags, order, d):
    spot = iota((1, HIDDEN), 1)
    order = order.astype(F32)

    def place(index, bit, count):
        value = jnp.sum(jnp.where(spot == index, order, 0.0), axis=1, keepdims=True)
        return (value.astype(jnp.int32) >> bit) & (count - 1)

    groups = (
        [place(d ^ k, 0, 2) for k in range(2)],
        [place(d ^ (k << 1), 1, 4) for k in range(4)],
        [place((d & 7) | (k << 3), 3, 4) for k in range(4)],
    )
    n = 0
    for group in groups:
        for i in range(len(group)):
            for j in range(i + 1, len(group)):
                flag = jnp.where(group[i] < group[j], 1.0, 0.0)
                flags[n] = jnp.broadcast_to(flag, (8, 128))
                n += 1


def keep_kernel(
    where, flags, feats, w1, w2, coverage, shift, received, *refs, step, slot
):
    out = refs[-1]
    d = where[0]
    march(feats.at[d & 1, ((d >> 1) & 3) ^ step], w1, w2, coverage, shift, out)
    if step == 0:
        return
    state = tuple(out[o] for o in range(4))
    other = tuple(received[slot, o] for o in range(4))
    merged = over((state, other), flags, 0)
    for o in range(4):
        out[o] = merged[o]


def merge_z_kernel(where, flags, received, part0, part1, part2, part3, out):
    d = where[0]
    parts = [tuple(p[o] for o in range(4)) for p in (part0, part1, part2, part3)]
    parts[0] = over((parts[0], tuple(received[0, o] for o in range(4))), flags, 0)
    merged = over(parts, flags, 1)
    odd = (d & 1) == 1
    for o in range(4):
        rows = [merged[o][k : k + 1] for k in range(8)]
        for t in range(4):
            before, after = (t - 1) % 4, (t + 1) % 4
            out[t, o] = jnp.concatenate(
                [
                    rows[t],
                    rows[4 + t],
                    jnp.where(odd, rows[before], rows[after]),
                    jnp.where(odd, rows[4 + before], rows[4 + after]),
                ],
                0,
            )


def merge_x_kernel(where, flags, parts, centre, extra):
    d = where[0]
    group = [tuple(parts[k, o] for o in range(4)) for k in range(4)]
    merged = over(group, flags, 7)
    boundary = ((d & 7) == 0) | ((d & 7) == 7)
    for o in range(3):
        centre[o] = merged[o][0:2]
        extra[o] = jnp.where(boundary, merged[o][2:4], merged[o][0:2])


def filter_kernel(where, weight, bias, beside, centre, apart, out):
    half = centre.shape[2]
    even = (where[0] & 1) == 0
    lane = iota((2, half), 1)
    sub = iota((2, half), 0)
    spread = lambda v: jnp.concatenate([jnp.broadcast_to(v, (2, 128))] * (half // 128), 1)
    sums = [spread(bias[:, o : o + 1]) for o in range(3)]
    for i in range(3):
        above = jnp.where(even, apart[i], beside[i])
        below = jnp.where(even, beside[i], apart[i])
        for a, row in enumerate((above, centre[i], below)):
            flipped = jnp.concatenate([row[1:2], row[0:1]], 0)
            left = jnp.where(
                lane == 0, jnp.where(sub == 1, pltpu.roll(flipped, 1, 1), 0.0), pltpu.roll(row, 1, 1)
            )
            right = jnp.where(
                lane == half - 1,
                jnp.where(sub == 0, pltpu.roll(flipped, half - 1, 1), 0.0),
                pltpu.roll(row, half - 1, 1),
            )
            for b, window in enumerate((left, row, right)):
                for o in range(3):
                    sums[o] = sums[o] + spread(weight[o, i, a : a + 1, b : b + 1]) * window
    for o in range(3):
        out[o, :, :half] = sums[o][0:1]
        out[o, :, half:] = sums[o][1:2]


VMEM = pl.BlockSpec(memory_space=pltpu.VMEM)
SMEM = pl.BlockSpec(memory_space=pltpu.SMEM)
ANY = pl.BlockSpec(memory_space=pl.ANY)


def call(kernel, name, outs, specs, *args, scratch=(), micros=1.0, aliases={}):
    return pl.pallas_call(
        kernel,
        out_shape=outs,
        in_specs=specs,
        out_specs=jax.tree.map(lambda _: VMEM, outs),
        scratch_shapes=scratch,
        input_output_aliases=aliases,
        compiler_params=pltpu.CompilerParams(vmem_limit_bytes=24 * 2**20),
        name=name,
        cost_estimate=pl.CostEstimate(
            flops=int(micros * 1e9), bytes_accessed=0, transcendentals=0
        ),
    )(*args)


def shape(dims, dtype=F32):
    return jax.ShapeDtypeStruct(dims, dtype)


def across_pairs(strips, depths):
    pairs = []
    for y in range(strips):
        for d in range(depths):
            x, low, target = d >> 3, d & 7, None
            if low == 7:
                target = (y, 8 * x) if x > 0 else (y + 1, 0)
            elif low == 0:
                target = (y, 8 * x + 7) if x < depths // 8 - 1 else (y - 1, d + 7)
            else:
                target = (y, d + 1 if d % 2 else d - 1)
            if 0 <= target[0] < strips:
                pairs.append((y * depths + d, target[0] * depths + target[1]))
    return pairs


def table_of(kind, *arrays):
    flat = [v.reshape(-1, v.shape[-1]).astype(kind) for v in arrays]
    rows = sum(v.shape[0] for v in flat)
    total, at = jnp.zeros((rows, HIDDEN), kind), 0
    for v in flat:
        n, width = v.shape
        total = total + jnp.pad(v, ((at, rows - at - n), (0, HIDDEN - width)))
        at += n
    return total


def shards(volume, occupancy, slab_order, w_in, b_in, w_out, b_out, conv_weight, conv_bias):
    strips = lax.axis_size("strip")
    depths = lax.axis_size("depth")
    layers, rows, columns = volume.shape
    half = columns // 2
    optical = 2.0 / (layers * depths)
    d = lax.axis_index("depth")
    where = d.astype(jnp.int32).reshape(1)
    facts = table_of(F32, w_in, b_in, w_out.T, b_out)
    counts = table_of(jnp.int32, occupancy, slab_order)
    top = lax.ppermute(volume[:, rows - 1 :], "strip", [(i, i + 1) for i in range(strips - 1)])
    bot = lax.ppermute(volume[:, :1], "strip", [(i + 1, i) for i in range(strips - 1)])
    feats, w1, w2, coverage, shift, flags = call(
        functools.partial(feature_kernel, optical=optical),
        "features",
        (
            shape((2, 4, layers, KDIM, half), BF16),
            shape((HIDDEN * 8, KDIM), BF16),
            shape((32, HIDDEN * 8), BF16),
            shape((8, half)),
            shape((32, 128)),
            shape((13, 8, 128)),
        ),
        [SMEM] + [VMEM] * 3,
        where,
        volume,
        facts,
        counts,
        scratch=[
            pltpu.VMEM((rows * columns // 128, 128), F32),
            pltpu.VMEM((layers, 8, 8, half), F32),
        ],
    )
    net = (w1, w2, coverage, shift)
    cores = [(i, i ^ 1) for i in range(depths)]
    feats = call(
        edge_kernel,
        "edges",
        shape(feats.shape, BF16),
        [VMEM] * 3,
        feats,
        top,
        bot,
        aliases={0: 0},
    )
    latest = shift

    def send(steps):
        return call(
            functools.partial(send_kernel, steps=steps),
            "march_send" + "".join(map(str, steps)),
            shape((len(steps), 4, 8, half)),
            [SMEM] + [VMEM] * 5 + [ANY],
            where,
            feats,
            *net,
            latest,
            micros=3.0 * len(steps),
        )

    def keep(step, received, slot, *landed):
        return call(
            functools.partial(keep_kernel, step=step, slot=slot),
            f"march_keep{step}",
            shape((4, 8, half)),
            [SMEM] + [VMEM] * 6 + [VMEM if step else ANY, ANY] + [ANY] * len(landed),
            where,
            flags,
            feats,
            *net,
            received,
            latest,
            *landed,
            micros=3.0,
        )

    received, parts = {}, [None] * 4
    for kind, steps in PLAN:
        if kind == "send":
            latest = send(steps)
            arriving = lax.ppermute(latest, "depth", cores)
            for slot, step in enumerate(steps):
                received[step] = (arriving, slot)
            continue
        for step in steps:
            landed = [parts[n] for n in AWAITED] if step == 0 else []
            latest = keep(step, *received[step if step else 3], *landed)
            parts[step] = latest
            if step:
                swap = [(i, i ^ (step << 1)) for i in range(depths)]
                parts[step] = lax.ppermute(latest, "depth", swap)
    rows_out = call(
        merge_z_kernel,
        "merge_z",
        shape((4, 4, 4, half)),
        [SMEM] + [VMEM] * 6,
        where,
        flags,
        received[0][0],
        *parts,
    )
    rows_in = lax.all_to_all(
        rows_out,
        "depth",
        0,
        0,
        tiled=True,
        axis_index_groups=[[i | (k << 3) for k in range(4)] for i in range(8)],
    )
    picture, extra = call(
        merge_x_kernel,
        "merge_x",
        (shape((3, 2, half)), shape((3, 2, half))),
        [SMEM, VMEM, VMEM],
        where,
        flags,
        rows_in,
    )
    apart = lax.ppermute(extra, ("strip", "depth"), across_pairs(strips, depths))
    beside = lax.ppermute(picture, "depth", cores)
    filtered = call(
        filter_kernel,
        "filter",
        shape((3, 1, columns)),
        [SMEM] + [VMEM] * 5,
        where,
        conv_weight,
        conv_bias.reshape(1, 3),
        beside,
        picture,
        apart,
    )
    return filtered.reshape(3, 1, 1, 1, columns)


def solution(mesh):
    placed = (
        P("depth", "strip", None),
        P("depth", "strip", None),
        P(),
        P(),
        P(),
        P(),
        P(),
        P(),
        P(),
    )
    return jax.shard_map(
        shards,
        mesh=mesh,
        in_specs=placed,
        out_specs=P(None, "strip", None, "depth", None),
        check_vma=False,
    )
```
